128 devices in a mesh: gx: 8 (over z, core), gy: 16 (over x, y).
Axes of the slice: x: 4, y: 4, z: 4, core: 2. Of those that a mesh axis runs over, the one named last changes fastest.
Arguments:
- part_column: int32 [128, 128, 256], P(('gx', 'gy')), may hold values from 0 to 127
- part_layer: int32 [128, 128, 256], P(('gx', 'gy')), may hold values from 0 to 255
- part_count: int32 [128, 128], P(('gx', 'gy')), may hold values from 0 to 256, as said below
- part_data: float32 [128, 128, 7, 256], P(('gx', 'gy')), may hold values from -8 to 8, as said below
- source: float32 [128, 128, 256], P('gx', 'gy'), may hold values from -14 to 14
Outputs:
- porosity: float32 [128, 128, 256], P('gx', 'gy')
- drag_momentum_field: float32 [3, 128, 128, 256], P(None, 'gx', 'gy')
- pressure: float32 [128, 128, 256], P('gx', 'gy')
The draws below stay inside these ranges and needn't reach their ends.
Inputs may be any that keep to these rules, and one draw needn't show every extreme that they name: `part_count`: slots of one source for one destination hold live particles first, then padding with arbitrary values; in every draw some destination device receives 256 particles from every source. `part_data`: rows 0 to 2 lie in [0, 1), row 3 is positive.
All inputs are finite; a program needn't handle non-finite values.
Results may differ from the reference program's by a relative error of at most 0.00013.
Values sent between devices are 32-bit elements; how exact they have to be, the bound alone decides.
A program may use at most 64 MiB of HBM per device.

```python
import jax
import jax.numpy as jnp
from jax import lax

CX = 16
CY = 8
NZ = 256
CAP = 256
ITERS = 3
NX = 128
NY = 128
N_GY = 16
DEVICES = 128


def draw_part_count(key, part):
    first_key, second_key = jax.random.split(key)
    counts = jax.random.randint(first_key, (DEVICES, DEVICES), 0, CAP + 1)
    busiest_device = jax.random.randint(second_key, (), 0, DEVICES)
    columns = lax.broadcasted_iota(jnp.int32, (DEVICES, DEVICES), 1)
    return jnp.where(columns == busiest_device, CAP, counts).astype(jnp.int32)


def draw_part_data(key, part):
    keys = jax.random.split(key, 3)
    offsets = jax.random.uniform(keys[0], (DEVICES, DEVICES, 3, CAP), jnp.float32, 0.0, 1.0)
    volumes = jnp.exp(jax.random.uniform(keys[1], (DEVICES, DEVICES, 1, CAP), jnp.float32, -2.9957, 0.0))
    drags = jnp.clip(jax.random.normal(keys[2], (DEVICES, DEVICES, 3, CAP), jnp.float32), -4.0, 4.0)
    return jnp.concatenate([offsets, volumes, drags], axis=2).astype(jnp.float32)


def draw_source(key, part):
    along_x = lax.broadcasted_iota(jnp.float32, (NX, NY, NZ), 0) / NX
    along_y = lax.broadcasted_iota(jnp.float32, (NX, NY, NZ), 1) / NY
    scales = 0.3 * 10.0 ** (0.5 * (along_x + along_y))
    random_part = jnp.clip(jax.random.normal(key, (NX, NY, NZ), jnp.float32), -4.0, 4.0)
    return (random_part * scales).astype(jnp.float32)


def touch_ends(values, own_key, low, high):
    longest = values.shape.index(max(values.shape))
    spots = []
    for shift in (0, 1):
        where = [jax.random.randint(jax.random.fold_in(own_key, axis), (), 0, length) for axis, length in enumerate(values.shape)]
        where[longest] = (where[longest] + shift) % values.shape[longest]
        spots.append(tuple(where))
    return values.at[spots[0]].set(low).at[spots[1]].set(high)


def setup_inputs(seed: int = 0) -> dict:
    streams_of = jax.random.split(jax.random.key(seed), 6)
    return {
        "part_column": touch_ends(jax.random.randint(streams_of[0], (DEVICES, DEVICES, CAP), 0, CX * CY), jax.random.fold_in(streams_of[0], 1), 0, (CX * CY) - 1).astype(jnp.int32),
        "part_layer": touch_ends(jax.random.randint(streams_of[1], (DEVICES, DEVICES, CAP), 0, NZ), jax.random.fold_in(streams_of[1], 1), 0, NZ - 1).astype(jnp.int32),
        "part_count": draw_part_count(jax.random.fold_in(streams_of[5], 71), 0),
        "part_data": draw_part_data(jax.random.fold_in(streams_of[5], 71), 0),
        "source": draw_source(jax.random.fold_in(streams_of[5], 71), 0),
    }


diag_shift = 0.01


def operate(values, stencil_weights):
    x_upper, x_lower, y_upper, y_lower, z_upper, z_lower = stencil_weights
    result = diag_shift * values
    result = result + x_upper * (values - jnp.roll(values, -1, 0))
    result = result + x_lower * (values - jnp.roll(values, 1, 0))
    result = result + y_upper * (values - jnp.roll(values, -1, 1))
    result = result + y_lower * (values - jnp.roll(values, 1, 1))
    result = result + z_upper * (values - jnp.roll(values, -1, 2))
    result = result + z_lower * (values - jnp.roll(values, 1, 2))
    return result


def reference(part_column, part_layer, part_count, part_data, source):
    slot_index = jnp.arange(CAP, dtype=jnp.int32)
    slot_live = (slot_index[None, None, :] < part_count[:, :, None]).astype(jnp.float32)
    owners = jnp.arange(DEVICES, dtype=jnp.int32)
    anchor_x = (owners // N_GY) * CX
    anchor_y = (owners % N_GY) * CY
    cell_x = anchor_x[None, :, None] + part_column // CY
    cell_y = anchor_y[None, :, None] + part_column % CY
    offset_x = part_data[:, :, 0]
    offset_y = part_data[:, :, 1]
    offset_z = part_data[:, :, 2]
    carried = part_data[:, :, 3:7] * slot_live[:, :, None, :]
    carried = jnp.moveaxis(carried, 2, 0).reshape(4, -1)
    deposit = jnp.zeros((4, NX * NY * NZ), jnp.float32)
    for corner in range(8):
        step_x, step_y, step_z = corner // 4, (corner // 2) % 2, corner % 2
        weight_x = offset_x if step_x else 1.0 - offset_x
        weight_y = offset_y if step_y else 1.0 - offset_y
        weight_z = offset_z if step_z else 1.0 - offset_z
        weight = (weight_x * weight_y * weight_z).reshape(-1)
        target = ((cell_x + step_x) % NX * NY + (cell_y + step_y) % NY) * NZ + (part_layer + step_z) % NZ
        deposit = deposit.at[:, target.reshape(-1)].add(carried * weight[None, :])
    deposit = deposit.reshape(4, NX, NY, NZ)
    porosity = 1.0 / (1.0 + deposit[0])
    drag_momentum_field = deposit[1:]
    divergence = 0.5 * (jnp.roll(drag_momentum_field[0], -1, 0) - jnp.roll(drag_momentum_field[0], 1, 0))
    divergence = divergence + 0.5 * (jnp.roll(drag_momentum_field[1], -1, 1) - jnp.roll(drag_momentum_field[1], 1, 1))
    divergence = divergence + 0.5 * (jnp.roll(drag_momentum_field[2], -1, 2) - jnp.roll(drag_momentum_field[2], 1, 2))
    right_side = source - divergence
    x_upper = 0.5 * (porosity + jnp.roll(porosity, -1, 0))
    x_lower = jnp.roll(x_upper, 1, 0)
    y_upper = 0.5 * (porosity + jnp.roll(porosity, -1, 1))
    y_lower = jnp.roll(y_upper, 1, 1)
    z_upper = 0.5 * (porosity + jnp.roll(porosity, -1, 2))
    z_lower = jnp.roll(z_upper, 1, 2)
    stencil_weights = (x_upper, x_lower, y_upper, y_lower, z_upper, z_lower)
    precond = 1.0 / (diag_shift + x_upper + x_lower + y_upper + y_lower + z_upper + z_lower)
    pressure = jnp.zeros_like(source)
    residual = right_side
    scaled = precond * residual
    direction = scaled
    product_now = jnp.sum(residual * scaled)
    for iteration in range(ITERS):
        applied = operate(direction, stencil_weights)
        step_size = product_now / jnp.sum(direction * applied)
        pressure = pressure + step_size * direction
        if iteration + 1 < ITERS:
            residual = residual - step_size * applied
            scaled = precond * residual
            product_next = jnp.sum(residual * scaled)
            direction = scaled + (product_next / product_now) * direction
            product_now = product_next
    return porosity, drag_momentum_field, pressure
```

```python
import jax
import jax.numpy as jnp
from jax import lax
from jax.experimental import pallas as pl
from jax.experimental.pallas import tpu as pltpu
from jax.sharding import PartitionSpec as P

diag_shift = 0.01
WX, WY, NZ, CAP = 16, 8, 256, 256
NGX, NGY = 8, 16
MAIN = (WX + 1) * 4 * WY
ROWS = MAIN + 80
VALUES = 9
f32, bf16 = jnp.float32, jnp.bfloat16
MESH = pl.DeviceIdType.MESH


def split(a):
    high = a.astype(bf16)
    return high, (a - high.astype(f32)).astype(bf16)


def tables(row):
    part = [row[:, CAP * i : CAP * (i + 1)] for i in range(VALUES)]
    column, bz = part[0].astype(jnp.int32), part[1].astype(jnp.int32)
    ox, oy, oz = part[2:5]
    bx, by = column >> 3, column & 7
    xi = lax.broadcasted_iota(jnp.int32, (72, CAP), 0) >> 2
    fi = lax.broadcasted_iota(jnp.int32, (8, CAP), 0) & 3
    loads = jnp.where(fi == 0, part[5], jnp.where(fi == 1, part[6], jnp.where(fi == 2, part[7], part[8])))
    wx = jnp.where(bx == xi, 1.0 - ox, jnp.where(bx + 1 == xi, ox, 0.0))
    xf = (wx.reshape(9, 8, CAP) * loads[None]).reshape(72, CAP)
    yi = lax.broadcasted_iota(jnp.int32, (8, CAP), 0)
    wy = jnp.where(by == yi, 1.0 - oy, jnp.where(by + 1 == yi, oy, 0.0))
    over = jnp.where(by == 7, oy, 0.0)
    main = (xf[:68, None, :] * wy[None]).reshape(MAIN, CAP)
    extra = jnp.concatenate([xf * over, jnp.zeros((8, CAP), f32)], 0)
    q = jnp.round(oz * 256.0) * (1.0 / 256.0)
    e = oz - q
    zi = lax.broadcasted_iota(jnp.int32, (NZ, CAP), 0)
    here, above = zi == bz, zi == ((bz + 1) & (NZ - 1))
    z_high = jnp.where(here, 1.0 - q, jnp.where(above, q, 0.0)).astype(bf16)
    z_low = jnp.where(here, -e, jnp.where(above, e, 0.0)).astype(bf16)
    return split(main), split(extra), (z_high, z_low)


def dot_nt(a, b):
    return lax.dot_general(a, b, (((1,), (1,)), ((), ())), preferred_element_type=f32)


GROUP = 8


def deposit_kernel(parts_ref, total_ref):
    total_ref[...] = jnp.zeros_like(total_ref)

    def step(i, carry):
        main, extra, layer = [], [], []
        for g in range(GROUP):
            (mh, ml), (eh, el), (zh, zl) = tables(parts_ref[i * GROUP + g])
            main += [mh, ml, mh]
            extra += [eh, el, eh]
            layer += [zh, zh, zl]
        right = jnp.concatenate(layer, 1)
        total_ref[:MAIN] += dot_nt(jnp.concatenate(main, 1), right)
        total_ref[MAIN:] += dot_nt(jnp.concatenate(extra, 1), right)
        return carry

    lax.fori_loop(0, parts_ref.shape[0] // GROUP, step, 0)


def deposit(parts):
    return pl.pallas_call(
        deposit_kernel,
        out_shape=jax.ShapeDtypeStruct((ROWS, NZ), f32),
        in_specs=[pl.BlockSpec(memory_space=pltpu.VMEM)],
        out_specs=pl.BlockSpec(memory_space=pltpu.VMEM),
        compiler_params=pltpu.CompilerParams(vmem_limit_bytes=48 << 20),
        name="deposit",
    )(parts)


def tail_kernel(
    total, source, porosity_out, drag_out, pressure_out,
    over_x, over_y, over_c, poro, face, y_send, y_recv, u0, u1, u2, red, red_x, red_y,
    over_send, over_recv, halo_send, halo_recv, rx_send, rx_recv, ry_send, ry_recv,
):
    gx, gy = lax.axis_index("gx"), lax.axis_index("gy")
    xp, xm = lax.rem(gx + 1, NGX), lax.rem(gx + NGX - 1, NGX)
    yp, ym = lax.rem(gy + 1, NGY), lax.rem(gy + NGY - 1, NGY)
    barrier = pltpu.get_barrier_semaphore()
    for k in range(1, NGX):
        pl.semaphore_signal(barrier, inc=1, device_id=(lax.rem(gx + k, NGX), gy), device_id_type=MESH)
    for k in range(1, NGY):
        pl.semaphore_signal(barrier, inc=1, device_id=(gx, lax.rem(gy + k, NGY)), device_id_type=MESH)
    pl.semaphore_signal(barrier, inc=1, device_id=(xp, yp), device_id_type=MESH)
    pl.semaphore_signal(barrier, inc=1, device_id=(xm, ym), device_id_type=MESH)
    pl.semaphore_wait(barrier, NGX + NGY)

    def send(src, dst, send_sem, recv_sem, to):
        copy = pltpu.make_async_remote_copy(
            src_ref=src, dst_ref=dst, send_sem=send_sem, recv_sem=recv_sem, device_id=to, device_id_type=MESH
        )
        copy.start()
        return copy

    copies = [
        send(total.at[pl.ds(512, 32)], over_x, over_send.at[0], over_recv.at[0], (xp, gy)),
        send(total.at[pl.ds(MAIN, 64)], over_y, over_send.at[1], over_recv.at[1], (gx, yp)),
        send(total.at[pl.ds(MAIN + 64, 8)], over_c, over_send.at[2], over_recv.at[2], (xp, yp)),
    ]
    for copy in copies:
        copy.wait()
    from_y = jnp.concatenate([over_y[:8] + over_c[...], over_y[8:]], 0)
    inner = total[:512].reshape(64, 8, NZ)
    inner = jnp.concatenate([inner[:4] + over_x[...].reshape(4, 8, NZ), inner[4:]], 0)
    row = lax.broadcasted_iota(jnp.int32, (64, 8, NZ), 1)
    inner = inner + jnp.where(row == 0, from_y[:, None, :], 0.0)
    inner = inner.reshape(WX, 4, 8, NZ)
    porosity = 1.0 / (1.0 + inner[:, 0])
    drag = [inner[:, 1], inner[:, 2], inner[:, 3]]
    porosity_out[...] = porosity
    for m in range(3):
        drag_out[m] = drag[m]

    poro[0, 1 : WX + 1] = porosity
    poro[1, 1 : WX + 1] = drag[0]

    def exchange(k, fields, y_faces):
        n = y_faces[0].shape[0]
        y_send[k, 0, :n] = y_faces[0]
        y_send[k, 1, :n] = y_faces[1]
        copies = [
            send(fields(WX), fields(0), halo_send.at[k, 0], halo_recv.at[k, 0], (xp, gy)),
            send(fields(1), fields(WX + 1), halo_send.at[k, 1], halo_recv.at[k, 1], (xm, gy)),
            send(y_send.at[k, 0, pl.ds(0, n)], y_recv.at[k, 0, pl.ds(0, n)], halo_send.at[k, 2], halo_recv.at[k, 2], (gx, yp)),
            send(y_send.at[k, 1, pl.ds(0, n)], y_recv.at[k, 1, pl.ds(0, n)], halo_send.at[k, 3], halo_recv.at[k, 3], (gx, ym)),
        ]
        for copy in copies:
            copy.wait()

    def y_faces(values):
        return tuple(jnp.stack([v[:, y] for v in values]) for y in (7, 0))

    exchange(0, lambda x: poro.at[pl.ds(0, 2), x], y_faces([porosity, drag[1]]))

    yi = lax.broadcasted_iota(jnp.int32, (WX, 8, NZ), 1)

    def y_next(v, k, i):
        return jnp.where(yi == 7, y_recv[k, 1, i][:, None, :], pltpu.roll(v, 7, 1))

    def y_previous(v, k, i):
        return jnp.where(yi == 0, y_recv[k, 0, i][:, None, :], pltpu.roll(v, 1, 1))

    def z_next(v):
        return pltpu.roll(v, NZ - 1, 2)

    def z_previous(v):
        return pltpu.roll(v, 1, 2)

    divergence = 0.5 * (poro[1, 2:] - poro[1, :WX])
    divergence = divergence + 0.5 * (y_next(drag[1], 0, 1) - y_previous(drag[1], 0, 1))
    divergence = divergence + 0.5 * (z_next(drag[2]) - z_previous(drag[2]))
    right_side = source[...] - divergence
    x_upper = 0.5 * (porosity + poro[0, 2:])
    x_lower = 0.5 * (poro[0, :WX] + porosity)
    y_upper = 0.5 * (porosity + y_next(porosity, 0, 0))
    y_lower = 0.5 * (y_previous(porosity, 0, 0) + porosity)
    z_upper = 0.5 * (porosity + z_next(porosity))
    z_lower = z_previous(z_upper)
    precond = 1.0 / (diag_shift + x_upper + x_lower + y_upper + y_lower + z_upper + z_lower)
    for i, weights in enumerate((x_upper, x_lower, y_upper, y_lower, z_upper, z_lower, precond)):
        face[i] = weights

    def operate(k, u):
        v = u[1 : WX + 1]
        exchange(k, lambda x: u.at[x], tuple(v[:, y][None] for y in (7, 0)))
        result = diag_shift * v
        result = result + face[0] * (v - u[2:])
        result = result + face[1] * (v - u[:WX])
        result = result + face[2] * (v - y_next(v, k, 0))
        result = result + face[3] * (v - y_previous(v, k, 0))
        result = result + face[4] * (v - z_next(v))
        result = result + face[5] * (v - z_previous(v))
        return v, result

    def partial_sum(a, b):
        product = jnp.sum(a * b, 0)
        return jnp.sum(product[:, :128] + product[:, 128:], 0, keepdims=True)

    start = precond * right_side
    u0[1 : WX + 1] = start
    moments = [partial_sum(right_side, start)]
    v0, a0 = operate(1, u0)
    v1 = face[6] * a0
    u1[1 : WX + 1] = v1
    moments += [partial_sum(v0, a0), partial_sum(v1, a0)]
    v1, a1 = operate(2, u1)
    v2 = face[6] * a1
    u2[1 : WX + 1] = v2
    moments += [partial_sum(v1, a1), partial_sum(v2, a1)]
    v2, a2 = operate(3, u2)
    moments += [partial_sum(v2, a2)]

    zero = jnp.zeros((2, 128), f32)
    mine = jnp.concatenate(moments + [zero], 0)
    red[0] = mine
    red_x[gx] = mine
    copies = [
        send(red.at[0], red_x.at[gx], rx_send.at[k], rx_recv.at[k], (lax.rem(gx + k, NGX), gy)) for k in range(1, NGX)
    ]
    for copy in copies:
        copy.wait()
    mine = jnp.sum(red_x[...], 0)
    red[1] = mine
    red_y[gy] = mine
    copies = [
        send(red.at[1], red_y.at[gy], ry_send.at[k], ry_recv.at[k], (gx, lax.rem(gy + k, NGY))) for k in range(1, NGY)
    ]
    for copy in copies:
        copy.wait()
    sums = jnp.sum(jnp.sum(red_y[...], 0), 1, keepdims=True)
    m0, m1, m2, m3, m4, m5 = [sums[i : i + 1] for i in range(6)]
    l21, l31 = m2 / m1, m3 / m1
    d2 = m3 - l21 * m2
    e32 = m4 - l31 * m2
    r1 = m1 - l21 * m0
    r2 = m2 - l31 * m0
    l32 = e32 / d2
    d3 = (m5 - l31 * m3) - l32 * e32
    c2 = (r2 - l32 * r1) / d3
    c1 = r1 / d2 - l32 * c2
    c0 = m0 / m1 - l21 * c1 - l31 * c2
    c0, c1, c2 = [c.reshape(1, 1, 1) for c in (c0, c1, c2)]
    pressure_out[...] = c0 * u0[1 : WX + 1] + c1 * u1[1 : WX + 1] + c2 * u2[1 : WX + 1]


def tail(total, source):
    vmem = pl.BlockSpec(memory_space=pltpu.VMEM)
    block = (WX, WY, NZ)
    padded = (WX + 2, WY, NZ)
    dma = pltpu.SemaphoreType.DMA
    return pl.pallas_call(
        tail_kernel,
        out_shape=(
            jax.ShapeDtypeStruct(block, f32),
            jax.ShapeDtypeStruct((3,) + block, f32),
            jax.ShapeDtypeStruct(block, f32),
        ),
        in_specs=[vmem, vmem],
        out_specs=(vmem, vmem, vmem),
        scratch_shapes=[
            pltpu.VMEM((32, NZ), f32),
            pltpu.VMEM((64, NZ), f32),
            pltpu.VMEM((8, NZ), f32),
            pltpu.VMEM((2,) + padded, f32),
            pltpu.VMEM((7,) + block, f32),
            pltpu.VMEM((4, 2, 2, WX, NZ), f32),
            pltpu.VMEM((4, 2, 2, WX, NZ), f32),
            pltpu.VMEM(padded, f32),
            pltpu.VMEM(padded, f32),
            pltpu.VMEM(padded, f32),
            pltpu.VMEM((2, 8, 128), f32),
            pltpu.VMEM((NGX, 8, 128), f32),
            pltpu.VMEM((NGY, 8, 128), f32),
            dma((3,)), dma((3,)), dma((4, 4)), dma((4, 4)),
            dma((NGX,)), dma((NGX,)), dma((NGY,)), dma((NGY,)),
        ],
        compiler_params=pltpu.CompilerParams(
            collective_id=0, has_side_effects=True, vmem_limit_bytes=48 << 20
        ),
        name="tail",
    )(total, source)


def shards(part_column, part_layer, part_count, part_data, source):
    live = lax.broadcasted_iota(jnp.int32, (1, 1, CAP), 2) < part_count[0][:, None, None]
    data = part_data[0]
    packed = jnp.concatenate(
        [
            part_column[0].astype(f32)[:, None],
            part_layer[0].astype(f32)[:, None],
            data[:, :3],
            jnp.where(live, data[:, 3:], 0.0),
        ],
        axis=1,
    ).reshape(-1, 1, VALUES * CAP)
    parts = lax.all_to_all(packed, ("gx", "gy"), split_axis=0, concat_axis=0, tiled=True)
    return tail(deposit(parts), source)


def solution(mesh):
    placed = (
        P(("gx", "gy"), None, None),
        P(("gx", "gy"), None, None),
        P(("gx", "gy"), None),
        P(("gx", "gy"), None, None, None),
        P("gx", "gy", None),
    )
    return jax.shard_map(
        shards,
        mesh=mesh,
        in_specs=placed,
        out_specs=(P("gx", "gy", None), P(None, "gx", "gy", None), P("gx", "gy", None)),
        check_vma=False,
    )
```

```python
import jax
import jax.numpy as jnp
from jax import lax
from jax.experimental import pallas as pl
from jax.experimental.pallas import tpu as pltpu
from jax.sharding import PartitionSpec as P

diag_shift = 0.01
WX, WY, NZ, CAP = 16, 8, 256, 256
NGX, NGY = 8, 16
MAIN = (WX + 1) * 4 * WY
ROWS = MAIN + 80
VALUES = 9
f32, bf16 = jnp.float32, jnp.bfloat16
MESH = pl.DeviceIdType.MESH


def tables(slot, k):
    part = [slot[k, i : i + 1] for i in range(VALUES)]
    ox, oy, oz = part[:3]
    column, bz = part[7].astype(jnp.int32), part[8].astype(jnp.int32)
    bx, by = column >> 3, column & 7
    xi = lax.broadcasted_iota(jnp.int32, (72, CAP), 0) >> 2
    fi = lax.broadcasted_iota(jnp.int32, (8, CAP), 0) & 3
    loads = jnp.where(fi == 0, part[3], jnp.where(fi == 1, part[4], jnp.where(fi == 2, part[5], part[6])))
    wx = jnp.where(bx == xi, 1.0 - ox, jnp.where(bx + 1 == xi, ox, 0.0))
    xf = (wx.reshape(9, 8, CAP) * loads[None]).reshape(72, CAP)
    yi = lax.broadcasted_iota(jnp.int32, (8, CAP), 0)
    wy = jnp.where(by == yi, 1.0 - oy, jnp.where(by + 1 == yi, oy, 0.0))
    over = jnp.where(by == 7, oy, 0.0)
    main = (xf[:68, None, :] * wy[None]).reshape(MAIN, CAP)
    left = jnp.concatenate([main, xf * over, jnp.zeros((8, CAP), f32)], 0)
    high = left.astype(bf16)
    low = (left - high.astype(f32)).astype(bf16)
    q = jnp.round(oz * 256.0) * (1.0 / 256.0)
    e = oz - q
    zi = lax.broadcasted_iota(jnp.int32, (NZ, CAP), 0)
    here, above = zi == bz, zi == ((bz + 1) & (NZ - 1))
    z_high = jnp.where(here, 1.0 - q, jnp.where(above, q, 0.0)).astype(bf16)
    z_low = jnp.where(here, -e, jnp.where(above, e, 0.0)).astype(bf16)
    return high, low, z_high, z_low


def dot_nt(a, b):
    return lax.dot_general(a, b, (((1,), (1,)), ((), ())), preferred_element_type=f32)


GROUP = 16
DEVICES = NGX * NGY


def kernel(
    counts, columns, layers, data, source, porosity_out, drag_out, pressure_out,
    packed, slots, total, all_send, all_recv,
    over_x, over_y, over_c, poro, face, y_send, y_recv, u0, u1, u2, red, red_x, red_y,
    over_send, over_recv, halo_send, halo_recv, rx_send, rx_recv, ry_send, ry_recv,
):
    gx, gy = lax.axis_index("gx"), lax.axis_index("gy")
    xp, xm = lax.rem(gx + 1, NGX), lax.rem(gx + NGX - 1, NGX)
    yp, ym = lax.rem(gy + 1, NGY), lax.rem(gy + NGY - 1, NGY)

    def peer(k):
        return lax.rem(gx + lax.rem(k, NGX), NGX), lax.rem(gy + lax.div(k, NGX), NGY)

    barrier = pltpu.get_barrier_semaphore()

    def greet(k, carry):
        pl.semaphore_signal(barrier, inc=1, device_id=peer(k), device_id_type=MESH)
        return carry

    lax.fori_loop(1, DEVICES, greet, 0)

    lane = lax.broadcasted_iota(jnp.int32, (8, CAP), 1)
    row = lax.broadcasted_iota(jnp.int32, (8, CAP), 0)

    def pack(d):
        live = lane < counts[0, d]
        values = jnp.concatenate([data[d], columns[pl.ds(d, 1)].astype(f32)], 0)
        return jnp.where(live | (row < 3) | (row == 7), values, 0.0), layers[pl.ds(d, 1)].astype(f32)

    own = gx * NGY + gy
    upper, lower = pack(own)
    slots[0, :8] = upper
    slots[0, 8:] = lower

    pl.semaphore_wait(barrier, DEVICES - 1)

    def ship(k, carry):
        px, py = peer(k)
        upper, lower = pack(px * NGY + py)
        packed[k, :8] = upper
        packed[k, 8:] = lower
        pltpu.make_async_remote_copy(
            src_ref=packed.at[k],
            dst_ref=slots.at[k],
            send_sem=all_send,
            recv_sem=all_recv.at[lax.div(k, GROUP)],
            device_id=(px, py),
            device_id_type=MESH,
        ).start()
        return carry

    lax.fori_loop(1, DEVICES, ship, 0)

    def arrived(group, first, count):
        block = slots.at[pl.ds(first, count)]
        pltpu.make_async_copy(block, block, all_recv.at[group]).wait()

    def add_group(i):
        left, right = [], []
        for g in range(GROUP):
            high, low, z_high, z_low = tables(slots, i * GROUP + g)
            left += [high, low, high]
            right += [z_high, z_high, z_low]
        return dot_nt(jnp.concatenate(left, 1), jnp.concatenate(right, 1))

    total[...] = jnp.zeros_like(total)

    def step(i, carry):
        @pl.when(i == 0)
        def _():
            arrived(0, 1, GROUP - 1)

        @pl.when(i > 0)
        def _():
            arrived(i, i * GROUP, GROUP)

        total[...] += add_group(i)
        return carry

    lax.fori_loop(0, DEVICES // GROUP, step, 0)
    shipped = packed.at[pl.ds(1, DEVICES - 1)]
    pltpu.make_async_copy(shipped, shipped, all_send).wait()

    def send(src, dst, send_sem, recv_sem, to):
        copy = pltpu.make_async_remote_copy(
            src_ref=src, dst_ref=dst, send_sem=send_sem, recv_sem=recv_sem, device_id=to, device_id_type=MESH
        )
        copy.start()
        return copy

    copies = [
        send(total.at[pl.ds(512, 32)], over_x, over_send.at[0], over_recv.at[0], (xp, gy)),
        send(total.at[pl.ds(MAIN, 64)], over_y, over_send.at[1], over_recv.at[1], (gx, yp)),
        send(total.at[pl.ds(MAIN + 64, 8)], over_c, over_send.at[2], over_recv.at[2], (xp, yp)),
    ]
    for copy in copies:
        copy.wait()
    from_y = jnp.concatenate([over_y[:8] + over_c[...], over_y[8:]], 0)
    inner = total[:512].reshape(64, 8, NZ)
    inner = jnp.concatenate([inner[:4] + over_x[...].reshape(4, 8, NZ), inner[4:]], 0)
    row = lax.broadcasted_iota(jnp.int32, (64, 8, NZ), 1)
    inner = inner + jnp.where(row == 0, from_y[:, None, :], 0.0)
    inner = inner.reshape(WX, 4, 8, NZ)
    porosity = 1.0 / (1.0 + inner[:, 0])
    drag = [inner[:, 1], inner[:, 2], inner[:, 3]]
    porosity_out[...] = porosity
    for m in range(3):
        drag_out[m] = drag[m]

    poro[0, 1 : WX + 1] = porosity
    poro[1, 1 : WX + 1] = drag[0]

    def exchange(k, fields, y_faces):
        n = y_faces[0].shape[0]
        y_send[k, 0, :n] = y_faces[0]
        y_send[k, 1, :n] = y_faces[1]
        copies = [
            send(fields(WX), fields(0), halo_send.at[k, 0], halo_recv.at[k, 0], (xp, gy)),
            send(fields(1), fields(WX + 1), halo_send.at[k, 1], halo_recv.at[k, 1], (xm, gy)),
            send(y_send.at[k, 0, pl.ds(0, n)], y_recv.at[k, 0, pl.ds(0, n)], halo_send.at[k, 2], halo_recv.at[k, 2], (gx, yp)),
            send(y_send.at[k, 1, pl.ds(0, n)], y_recv.at[k, 1, pl.ds(0, n)], halo_send.at[k, 3], halo_recv.at[k, 3], (gx, ym)),
        ]
        for copy in copies:
            copy.wait()

    def y_faces(values):
        return tuple(jnp.stack([v[:, y] for v in values]) for y in (7, 0))

    exchange(0, lambda x: poro.at[pl.ds(0, 2), x], y_faces([porosity, drag[1]]))

    yi = lax.broadcasted_iota(jnp.int32, (WX, 8, NZ), 1)

    def y_next(v, k, i):
        return jnp.where(yi == 7, y_recv[k, 1, i][:, None, :], pltpu.roll(v, 7, 1))

    def y_previous(v, k, i):
        return jnp.where(yi == 0, y_recv[k, 0, i][:, None, :], pltpu.roll(v, 1, 1))

    def z_next(v):
        return pltpu.roll(v, NZ - 1, 2)

    def z_previous(v):
        return pltpu.roll(v, 1, 2)

    divergence = 0.5 * (poro[1, 2:] - poro[1, :WX])
    divergence = divergence + 0.5 * (y_next(drag[1], 0, 1) - y_previous(drag[1], 0, 1))
    divergence = divergence + 0.5 * (z_next(drag[2]) - z_previous(drag[2]))
    right_side = source[...] - divergence
    x_upper = 0.5 * (porosity + poro[0, 2:])
    x_lower = 0.5 * (poro[0, :WX] + porosity)
    y_upper = 0.5 * (porosity + y_next(porosity, 0, 0))
    y_lower = 0.5 * (y_previous(porosity, 0, 0) + porosity)
    z_upper = 0.5 * (porosity + z_next(porosity))
    z_lower = z_previous(z_upper)
    precond = 1.0 / (diag_shift + x_upper + x_lower + y_upper + y_lower + z_upper + z_lower)
    for i, weights in enumerate((x_upper, x_lower, y_upper, y_lower, z_upper, z_lower, precond)):
        face[i] = weights

    def operate(k, u):
        v = u[1 : WX + 1]
        exchange(k, lambda x: u.at[x], tuple(v[:, y][None] for y in (7, 0)))
        result = diag_shift * v
        result = result + face[0] * (v - u[2:])
        result = result + face[1] * (v - u[:WX])
        result = result + face[2] * (v - y_next(v, k, 0))
        result = result + face[3] * (v - y_previous(v, k, 0))
        result = result + face[4] * (v - z_next(v))
        result = result + face[5] * (v - z_previous(v))
        return v, result

    def partial_sum(a, b):
        product = jnp.sum(a * b, 0)
        return jnp.sum(product[:, :128] + product[:, 128:], 0, keepdims=True)

    start = precond * right_side
    u0[1 : WX + 1] = start
    moments = [partial_sum(right_side, start)]
    v0, a0 = operate(1, u0)
    v1 = face[6] * a0
    u1[1 : WX + 1] = v1
    moments += [partial_sum(v0, a0), partial_sum(v1, a0)]
    v1, a1 = operate(2, u1)
    v2 = face[6] * a1
    u2[1 : WX + 1] = v2
    moments += [partial_sum(v1, a1), partial_sum(v2, a1)]
    v2, a2 = operate(3, u2)
    moments += [partial_sum(v2, a2)]

    zero = jnp.zeros((2, 128), f32)
    mine = jnp.concatenate(moments + [zero], 0)
    red[0] = mine
    red_x[gx] = mine
    copies = [
        send(red.at[0], red_x.at[gx], rx_send.at[k], rx_recv.at[k], (lax.rem(gx + k, NGX), gy)) for k in range(1, NGX)
    ]
    for copy in copies:
        copy.wait()
    mine = jnp.sum(red_x[...], 0)
    red[1] = mine
    red_y[gy] = mine
    copies = [
        send(red.at[1], red_y.at[gy], ry_send.at[k], ry_recv.at[k], (gx, lax.rem(gy + k, NGY))) for k in range(1, NGY)
    ]
    for copy in copies:
        copy.wait()
    sums = jnp.sum(jnp.sum(red_y[...], 0), 1, keepdims=True)
    m0, m1, m2, m3, m4, m5 = [sums[i : i + 1] for i in range(6)]
    l21, l31 = m2 / m1, m3 / m1
    d2 = m3 - l21 * m2
    e32 = m4 - l31 * m2
    r1 = m1 - l21 * m0
    r2 = m2 - l31 * m0
    l32 = e32 / d2
    d3 = (m5 - l31 * m3) - l32 * e32
    c2 = (r2 - l32 * r1) / d3
    c1 = r1 / d2 - l32 * c2
    c0 = m0 / m1 - l21 * c1 - l31 * c2
    c0, c1, c2 = [c.reshape(1, 1, 1) for c in (c0, c1, c2)]
    pressure_out[...] = c0 * u0[1 : WX + 1] + c1 * u1[1 : WX + 1] + c2 * u2[1 : WX + 1]


def run(counts, columns, layers, data, source):
    vmem = pl.BlockSpec(memory_space=pltpu.VMEM)
    block = (WX, WY, NZ)
    padded = (WX + 2, WY, NZ)
    dma = pltpu.SemaphoreType.DMA
    return pl.pallas_call(
        kernel,
        out_shape=(
            jax.ShapeDtypeStruct(block, f32),
            jax.ShapeDtypeStruct((3,) + block, f32),
            jax.ShapeDtypeStruct(block, f32),
        ),
        in_specs=[pl.BlockSpec(memory_space=pltpu.SMEM), vmem, vmem, vmem, vmem],
        out_specs=(vmem, vmem, vmem),
        scratch_shapes=[
            pltpu.VMEM((DEVICES, VALUES, CAP), f32),
            pltpu.VMEM((DEVICES, VALUES, CAP), f32),
            pltpu.VMEM((ROWS, NZ), f32),
            dma(()), dma((DEVICES // GROUP,)),
            pltpu.VMEM((32, NZ), f32),
            pltpu.VMEM((64, NZ), f32),
            pltpu.VMEM((8, NZ), f32),
            pltpu.VMEM((2,) + padded, f32),
            pltpu.VMEM((7,) + block, f32),
            pltpu.VMEM((4, 2, 2, WX, NZ), f32),
            pltpu.VMEM((4, 2, 2, WX, NZ), f32),
            pltpu.VMEM(padded, f32),
            pltpu.VMEM(padded, f32),
            pltpu.VMEM(padded, f32),
            pltpu.VMEM((2, 8, 128), f32),
            pltpu.VMEM((NGX, 8, 128), f32),
            pltpu.VMEM((NGY, 8, 128), f32),
            dma((3,)), dma((3,)), dma((4, 4)), dma((4, 4)),
            dma((NGX,)), dma((NGX,)), dma((NGY,)), dma((NGY,)),
        ],
        compiler_params=pltpu.CompilerParams(
            collective_id=0, has_side_effects=True, vmem_limit_bytes=48 << 20
        ),
        name="coupling",
    )(counts, columns, layers, data, source)


def shards(part_column, part_layer, part_count, part_data, source):
    return run(part_count, part_column[0], part_layer[0], part_data[0], source)


def solution(mesh):
    placed = (
        P(("gx", "gy"), None, None),
        P(("gx", "gy"), None, None),
        P(("gx", "gy"), None),
        P(("gx", "gy"), None, None, None),
        P("gx", "gy", None),
    )
    return jax.shard_map(
        shards,
        mesh=mesh,
        in_specs=placed,
        out_specs=(P("gx", "gy", None), P(None, "gx", "gy", None), P("gx", "gy", None)),
        check_vma=False,
    )
```

```python
import jax
import jax.numpy as jnp
from jax import lax
from jax.experimental import pallas as pl
from jax.experimental.pallas import tpu as pltpu
from jax.sharding import PartitionSpec as P

diag_shift = 0.01
WX, WY, NZ, CAP = 16, 8, 256, 256
NGX, NGY = 8, 16
MAIN = (WX + 1) * 4 * WY
ROWS = MAIN + 80
VALUES = 9
f32, bf16 = jnp.float32, jnp.bfloat16
MESH = pl.DeviceIdType.MESH


def tables(slot, k):
    part = [slot[k, :, CAP * i : CAP * (i + 1)] for i in range(VALUES)]
    ox, oy, oz = part[:3]
    column, bz = part[7].astype(jnp.int32), part[8].astype(jnp.int32)
    bx, by = column >> 3, column & 7
    xi = lax.broadcasted_iota(jnp.int32, (72, CAP), 0) >> 2
    fi = lax.broadcasted_iota(jnp.int32, (8, CAP), 0) & 3
    loads = jnp.where(fi == 0, part[3], jnp.where(fi == 1, part[4], jnp.where(fi == 2, part[5], part[6])))
    wx = jnp.where(bx == xi, 1.0 - ox, jnp.where(bx + 1 == xi, ox, 0.0))
    xf = (wx.reshape(9, 8, CAP) * loads[None]).reshape(72, CAP)
    yi = lax.broadcasted_iota(jnp.int32, (8, CAP), 0)
    wy = jnp.where(by == yi, 1.0 - oy, jnp.where(by + 1 == yi, oy, 0.0))
    over = jnp.where(by == 7, oy, 0.0)
    main = (xf[:68, None, :] * wy[None]).reshape(MAIN, CAP)
    left = jnp.concatenate([main, xf * over, jnp.zeros((8, CAP), f32)], 0)
    high = left.astype(bf16)
    low = (left - high.astype(f32)).astype(bf16)
    q = jnp.round(oz * 256.0) * (1.0 / 256.0)
    e = oz - q
    zi = lax.broadcasted_iota(jnp.int32, (NZ, CAP), 0)
    here, above = zi == bz, zi == ((bz + 1) & (NZ - 1))
    z_high = jnp.where(here, 1.0 - q, jnp.where(above, q, 0.0)).astype(bf16)
    z_low = jnp.where(here, -e, jnp.where(above, e, 0.0)).astype(bf16)
    return high, low, z_high, z_low


def dot_nt(a, b):
    return lax.dot_general(a, b, (((1,), (1,)), ((), ())), preferred_element_type=f32)


GROUP = 8
AHEAD = 4
DEVICES = NGX * NGY


def kernel(
    counts, columns, layers, data, source, porosity_out, drag_out, pressure_out,
    packed, slots, total, all_send, all_recv,
    over_x, over_y, over_c, poro, face, y_send, y_recv, u0, u1, u2, red, red_x, red_y,
    over_send, over_recv, halo_send, halo_recv, rx_send, rx_recv, ry_send, ry_recv,
):
    gx, gy = lax.axis_index("gx"), lax.axis_index("gy")
    xp, xm = lax.rem(gx + 1, NGX), lax.rem(gx + NGX - 1, NGX)
    yp, ym = lax.rem(gy + 1, NGY), lax.rem(gy + NGY - 1, NGY)

    def peer(k):
        return lax.rem(gx + lax.rem(k, NGX), NGX), lax.rem(gy + lax.div(k, NGX), NGY)

    barrier = pltpu.get_barrier_semaphore()

    lane = lax.broadcasted_iota(jnp.int32, (1, CAP), 1)

    def pack(target, k, d):
        live = lane < counts[0, d]
        rows = data[d]
        for i in range(7):
            row = rows[i : i + 1]
            target[k, :, CAP * i : CAP * (i + 1)] = row if i < 3 else jnp.where(live, row, 0.0)
        target[k, :, CAP * 7 : CAP * 8] = columns[pl.ds(d, 1)].astype(f32)
        target[k, :, CAP * 8 :] = layers[pl.ds(d, 1)].astype(f32)

    def greet(k, carry):
        px, py = peer(k)
        pl.semaphore_signal(barrier, inc=1, device_id=(px, py), device_id_type=MESH)
        pack(packed, k, px * NGY + py)
        return carry

    lax.fori_loop(1, DEVICES, greet, 0)
    pack(slots, 0, gx * NGY + gy)
    pl.semaphore_wait(barrier, DEVICES - 1)

    def ship(group, g):
        k = group * GROUP + g
        pltpu.make_async_remote_copy(
            src_ref=packed.at[k],
            dst_ref=slots.at[k],
            send_sem=all_send,
            recv_sem=all_recv.at[group],
            device_id=peer(k),
            device_id_type=MESH,
        ).start()

    for group in range(AHEAD):
        for g in range(GROUP):
            if group + g > 0:
                ship(group, g)

    def arrived(group, first, count):
        block = slots.at[pl.ds(first, count)]
        pltpu.make_async_copy(block, block, all_recv.at[group]).wait()

    def add_group(i):
        left, right = [], []
        for g in range(GROUP):
            high, low, z_high, z_low = tables(slots, i * GROUP + g)
            left += [high, low, high]
            right += [z_high, z_high, z_low]
        return dot_nt(jnp.concatenate(left, 1), jnp.concatenate(right, 1))

    total[...] = jnp.zeros_like(total)

    def step(i, shipping):
        @pl.when(i == 0)
        def _():
            arrived(0, 1, GROUP - 1)

        @pl.when(i > 0)
        def _():
            arrived(i, i * GROUP, GROUP)

        if shipping:
            for g in range(GROUP):
                ship(i + AHEAD, g)
        total[...] += add_group(i)

    groups = DEVICES // GROUP
    lax.fori_loop(0, groups - AHEAD, lambda i, c: (step(i, True), c)[1], 0)
    lax.fori_loop(groups - AHEAD, groups, lambda i, c: (step(i, False), c)[1], 0)
    shipped = packed.at[pl.ds(1, DEVICES - 1)]
    pltpu.make_async_copy(shipped, shipped, all_send).wait()

    def send(src, dst, send_sem, recv_sem, to):
        copy = pltpu.make_async_remote_copy(
            src_ref=src, dst_ref=dst, send_sem=send_sem, recv_sem=recv_sem, device_id=to, device_id_type=MESH
        )
        copy.start()
        return copy

    copies = [
        send(total.at[pl.ds(512, 32)], over_x, over_send.at[0], over_recv.at[0], (xp, gy)),
        send(total.at[pl.ds(MAIN, 64)], over_y, over_send.at[1], over_recv.at[1], (gx, yp)),
        send(total.at[pl.ds(MAIN + 64, 8)], over_c, over_send.at[2], over_recv.at[2], (xp, yp)),
    ]
    for copy in copies:
        copy.wait()
    from_y = jnp.concatenate([over_y[:8] + over_c[...], over_y[8:]], 0)
    inner = total[:512].reshape(64, 8, NZ)
    inner = jnp.concatenate([inner[:4] + over_x[...].reshape(4, 8, NZ), inner[4:]], 0)
    row = lax.broadcasted_iota(jnp.int32, (64, 8, NZ), 1)
    inner = inner + jnp.where(row == 0, from_y[:, None, :], 0.0)
    inner = inner.reshape(WX, 4, 8, NZ)
    porosity = 1.0 / (1.0 + inner[:, 0])
    drag = [inner[:, 1], inner[:, 2], inner[:, 3]]
    porosity_out[...] = porosity
    for m in range(3):
        drag_out[m] = drag[m]

    poro[0, 1 : WX + 1] = porosity
    poro[1, 1 : WX + 1] = drag[0]

    def exchange(k, fields, y_faces):
        n = y_faces[0].shape[0]
        y_send[k, 0, :n] = y_faces[0]
        y_send[k, 1, :n] = y_faces[1]
        copies = [
            send(fields(WX), fields(0), halo_send.at[k, 0], halo_recv.at[k, 0], (xp, gy)),
            send(fields(1), fields(WX + 1), halo_send.at[k, 1], halo_recv.at[k, 1], (xm, gy)),
            send(y_send.at[k, 0, pl.ds(0, n)], y_recv.at[k, 0, pl.ds(0, n)], halo_send.at[k, 2], halo_recv.at[k, 2], (gx, yp)),
            send(y_send.at[k, 1, pl.ds(0, n)], y_recv.at[k, 1, pl.ds(0, n)], halo_send.at[k, 3], halo_recv.at[k, 3], (gx, ym)),
        ]
        for copy in copies:
            copy.wait()

    def y_faces(values):
        return tuple(jnp.stack([v[:, y] for v in values]) for y in (7, 0))

    exchange(0, lambda x: poro.at[pl.ds(0, 2), x], y_faces([porosity, drag[1]]))

    yi = lax.broadcasted_iota(jnp.int32, (WX, 8, NZ), 1)

    def y_next(v, k, i):
        return jnp.where(yi == 7, y_recv[k, 1, i][:, None, :], pltpu.roll(v, 7, 1))

    def y_previous(v, k, i):
        return jnp.where(yi == 0, y_recv[k, 0, i][:, None, :], pltpu.roll(v, 1, 1))

    def z_next(v):
        return pltpu.roll(v, NZ - 1, 2)

    def z_previous(v):
        return pltpu.roll(v, 1, 2)

    divergence = 0.5 * (poro[1, 2:] - poro[1, :WX])
    divergence = divergence + 0.5 * (y_next(drag[1], 0, 1) - y_previous(drag[1], 0, 1))
    divergence = divergence + 0.5 * (z_next(drag[2]) - z_previous(drag[2]))
    right_side = source[...] - divergence
    x_upper = 0.5 * (porosity + poro[0, 2:])
    x_lower = 0.5 * (poro[0, :WX] + porosity)
    y_upper = 0.5 * (porosity + y_next(porosity, 0, 0))
    y_lower = 0.5 * (y_previous(porosity, 0, 0) + porosity)
    z_upper = 0.5 * (porosity + z_next(porosity))
    z_lower = z_previous(z_upper)
    precond = 1.0 / (diag_shift + x_upper + x_lower + y_upper + y_lower + z_upper + z_lower)
    for i, weights in enumerate((x_upper, x_lower, y_upper, y_lower, z_upper, z_lower, precond)):
        face[i] = weights

    def operate(k, u):
        v = u[1 : WX + 1]
        exchange(k, lambda x: u.at[x], tuple(v[:, y][None] for y in (7, 0)))
        result = diag_shift * v
        result = result + face[0] * (v - u[2:])
        result = result + face[1] * (v - u[:WX])
        result = result + face[2] * (v - y_next(v, k, 0))
        result = result + face[3] * (v - y_previous(v, k, 0))
        result = result + face[4] * (v - z_next(v))
        result = result + face[5] * (v - z_previous(v))
        return v, result

    def partial_sum(a, b):
        product = jnp.sum(a * b, 0)
        return jnp.sum(product[:, :128] + product[:, 128:], 0, keepdims=True)

    start = precond * right_side
    u0[1 : WX + 1] = start
    moments = [partial_sum(right_side, start)]
    v0, a0 = operate(1, u0)
    v1 = face[6] * a0
    u1[1 : WX + 1] = v1
    moments += [partial_sum(v0, a0), partial_sum(v1, a0)]
    v1, a1 = operate(2, u1)
    v2 = face[6] * a1
    u2[1 : WX + 1] = v2
    moments += [partial_sum(v1, a1), partial_sum(v2, a1)]
    v2, a2 = operate(3, u2)
    moments += [partial_sum(v2, a2)]

    zero = jnp.zeros((2, 128), f32)
    mine = jnp.concatenate(moments + [zero], 0)
    red[0] = mine
    red_x[gx] = mine
    copies = [
        send(red.at[0], red_x.at[gx], rx_send.at[k], rx_recv.at[k], (lax.rem(gx + k, NGX), gy)) for k in range(1, NGX)
    ]
    for copy in copies:
        copy.wait()
    mine = jnp.sum(red_x[...], 0)
    red[1] = mine
    red_y[gy] = mine
    copies = [
        send(red.at[1], red_y.at[gy], ry_send.at[k], ry_recv.at[k], (gx, lax.rem(gy + k, NGY))) for k in range(1, NGY)
    ]
    for copy in copies:
        copy.wait()
    sums = jnp.sum(jnp.sum(red_y[...], 0), 1, keepdims=True)
    m0, m1, m2, m3, m4, m5 = [sums[i : i + 1] for i in range(6)]
    l21, l31 = m2 / m1, m3 / m1
    d2 = m3 - l21 * m2
    e32 = m4 - l31 * m2
    r1 = m1 - l21 * m0
    r2 = m2 - l31 * m0
    l32 = e32 / d2
    d3 = (m5 - l31 * m3) - l32 * e32
    c2 = (r2 - l32 * r1) / d3
    c1 = r1 / d2 - l32 * c2
    c0 = m0 / m1 - l21 * c1 - l31 * c2
    c0, c1, c2 = [c.reshape(1, 1, 1) for c in (c0, c1, c2)]
    pressure_out[...] = c0 * u0[1 : WX + 1] + c1 * u1[1 : WX + 1] + c2 * u2[1 : WX + 1]


def run(counts, columns, layers, data, source):
    vmem = pl.BlockSpec(memory_space=pltpu.VMEM)
    block = (WX, WY, NZ)
    padded = (WX + 2, WY, NZ)
    dma = pltpu.SemaphoreType.DMA
    return pl.pallas_call(
        kernel,
        out_shape=(
            jax.ShapeDtypeStruct(block, f32),
            jax.ShapeDtypeStruct((3,) + block, f32),
            jax.ShapeDtypeStruct(block, f32),
        ),
        in_specs=[pl.BlockSpec(memory_space=pltpu.SMEM), vmem, vmem, vmem, vmem],
        out_specs=(vmem, vmem, vmem),
        scratch_shapes=[
            pltpu.VMEM((DEVICES, 1, VALUES * CAP), f32),
            pltpu.VMEM((DEVICES, 1, VALUES * CAP), f32),
            pltpu.VMEM((ROWS, NZ), f32),
            dma(()), dma((DEVICES // GROUP,)),
            pltpu.VMEM((32, NZ), f32),
            pltpu.VMEM((64, NZ), f32),
            pltpu.VMEM((8, NZ), f32),
            pltpu.VMEM((2,) + padded, f32),
            pltpu.VMEM((7,) + block, f32),
            pltpu.VMEM((4, 2, 2, WX, NZ), f32),
            pltpu.VMEM((4, 2, 2, WX, NZ), f32),
            pltpu.VMEM(padded, f32),
            pltpu.VMEM(padded, f32),
            pltpu.VMEM(padded, f32),
            pltpu.VMEM((2, 8, 128), f32),
            pltpu.VMEM((NGX, 8, 128), f32),
            pltpu.VMEM((NGY, 8, 128), f32),
            dma((3,)), dma((3,)), dma((4, 4)), dma((4, 4)),
            dma((NGX,)), dma((NGX,)), dma((NGY,)), dma((NGY,)),
        ],
        compiler_params=pltpu.CompilerParams(
            collective_id=0, has_side_effects=True, vmem_limit_bytes=48 << 20
        ),
        name="coupling",
    )(counts, columns, layers, data, source)


def shards(part_column, part_layer, part_count, part_data, source):
    return run(part_count, part_column[0], part_layer[0], part_data[0], source)


def solution(mesh):
    placed = (
        P(("gx", "gy"), None, None),
        P(("gx", "gy"), None, None),
        P(("gx", "gy"), None),
        P(("gx", "gy"), None, None, None),
        P("gx", "gy", None),
    )
    return jax.shard_map(
        shards,
        mesh=mesh,
        in_specs=placed,
        out_specs=(P("gx", "gy", None), P(None, "gx", "gy", None), P("gx", "gy", None)),
        check_vma=False,
    )
```

```python
import jax
import jax.numpy as jnp
from jax import lax
from jax.experimental import pallas as pl
from jax.experimental.pallas import tpu as pltpu
from jax.sharding import PartitionSpec as P

diag_shift = 0.01
WX, WY, NZ, CAP = 16, 8, 256, 256
NGX, NGY = 8, 16
MAIN = (WX + 1) * 4 * WY
ROWS = MAIN + 80
VALUES = 9
f32, bf16 = jnp.float32, jnp.bfloat16
MESH = pl.DeviceIdType.MESH


def tables(slot, k):
    part = [slot[k, :, CAP * i : CAP * (i + 1)] for i in range(VALUES)]
    ox, oy, oz = part[:3]
    column = part[7].astype(jnp.int32)
    bx, by = column >> 3, column & 7
    xi = lax.broadcasted_iota(jnp.int32, (72, CAP), 0) >> 2
    fi = lax.broadcasted_iota(jnp.int32, (8, CAP), 0) & 3
    loads = jnp.where(fi == 0, part[3], jnp.where(fi == 1, part[4], jnp.where(fi == 2, part[5], part[6])))
    wx = jnp.where(bx == xi, 1.0 - ox, jnp.where(bx + 1 == xi, ox, 0.0))
    xf = (wx.reshape(9, 8, CAP) * loads[None]).reshape(72, CAP)
    yi = lax.broadcasted_iota(jnp.int32, (8, CAP), 0)
    wy = jnp.where(by == yi, 1.0 - oy, jnp.where(by + 1 == yi, oy, 0.0))
    over = jnp.where(by == 7, oy, 0.0)
    main = (xf[:68, None, :] * wy[None]).reshape(MAIN, CAP)
    left = jnp.concatenate([main, xf * over, jnp.zeros((8, CAP), f32)], 0)
    high = left.astype(bf16)
    low = (left - high.astype(f32)).astype(bf16)
    q = jnp.round(oz * 256.0) * (1.0 / 256.0)
    e = oz - q
    zi = lax.broadcasted_iota(jnp.int32, (NZ, CAP), 0).astype(f32).astype(bf16)
    here = zi == part[8].astype(bf16)
    above = zi == jnp.where(part[8] == NZ - 1.0, 0.0, part[8] + 1.0).astype(bf16)
    zero = jnp.zeros((), bf16)
    rest = e.astype(bf16)
    z_high = jnp.where(here, (1.0 - q).astype(bf16), jnp.where(above, q.astype(bf16), zero))
    z_low = jnp.where(here, -rest, jnp.where(above, rest, zero))
    return high, low, z_high, z_low


def dot_nt(a, b):
    return lax.dot_general(a, b, (((1,), (1,)), ((), ())), preferred_element_type=f32)


GROUP = 8
HALO = 3
WIDE = WX + 2 * HALO
AHEAD = 4
DEVICES = NGX * NGY


def kernel(
    counts, columns, layers, data, source, porosity_out, drag_out, pressure_out,
    packed, slots, total, all_send, all_recv,
    over_x, over_y, over_c, dx_face, dy_send, dy_recv, y_send, y_recv, corner, face, poro, u0, u1, u2,
    red, red_x, red_y, over_send, over_recv, dx_send, dx_recv, halo_send, halo_recv, rx_send, rx_recv, ry_send, ry_recv,
):
    gx, gy = lax.axis_index("gx"), lax.axis_index("gy")
    xp, xm = lax.rem(gx + 1, NGX), lax.rem(gx + NGX - 1, NGX)
    yp, ym = lax.rem(gy + 1, NGY), lax.rem(gy + NGY - 1, NGY)

    def peer(k):
        return lax.rem(gx + lax.rem(k, NGX), NGX), lax.rem(gy + lax.div(k, NGX), NGY)

    barrier = pltpu.get_barrier_semaphore()

    lane = lax.broadcasted_iota(jnp.int32, (1, CAP), 1)

    def pack(target, k, d):
        live = lane < counts[0, d]
        rows = data[d]
        for i in range(7):
            row = rows[i : i + 1]
            target[k, :, CAP * i : CAP * (i + 1)] = row if i < 3 else jnp.where(live, row, 0.0)
        target[k, :, CAP * 7 : CAP * 8] = columns[pl.ds(d, 1)].astype(f32)
        target[k, :, CAP * 8 :] = layers[pl.ds(d, 1)].astype(f32)

    def greet(k, carry):
        pl.semaphore_signal(barrier, inc=1, device_id=peer(k), device_id_type=MESH)
        return carry

    def pack_one(k, carry):
        px, py = peer(k)
        pack(packed, k, px * NGY + py)
        return carry

    def greet_and_pack(k, carry):
        return pack_one(k, greet(k, carry))

    lax.fori_loop(1, AHEAD * GROUP, greet_and_pack, 0)
    lax.fori_loop(AHEAD * GROUP, DEVICES, greet, 0)
    pack(slots, 0, gx * NGY + gy)
    pl.semaphore_wait(barrier, DEVICES - 1)

    def ship(group, g):
        k = group * GROUP + g
        pltpu.make_async_remote_copy(
            src_ref=packed.at[k],
            dst_ref=slots.at[k],
            send_sem=all_send,
            recv_sem=all_recv.at[group],
            device_id=peer(k),
            device_id_type=MESH,
        ).start()

    for group in range(AHEAD):
        for g in range(GROUP):
            if group + g > 0:
                ship(group, g)

    def arrived(group, first, count):
        block = slots.at[pl.ds(first, count)]
        pltpu.make_async_copy(block, block, all_recv.at[group]).wait()

    def add_group(i):
        left, right = [], []
        for g in range(GROUP):
            high, low, z_high, z_low = tables(slots, i * GROUP + g)
            left += [high, low, high]
            right += [z_high, z_high, z_low]
        return dot_nt(jnp.concatenate(left, 1), jnp.concatenate(right, 1))

    total[...] = jnp.zeros_like(total)

    def step(i, shipping):
        @pl.when(i == 0)
        def _():
            arrived(0, 1, GROUP - 1)

        @pl.when(i > 0)
        def _():
            arrived(i, i * GROUP, GROUP)

        if shipping:
            for g in range(GROUP):
                pack_one((i + AHEAD) * GROUP + g, 0)
                ship(i + AHEAD, g)
        total[...] += add_group(i)

    groups = DEVICES // GROUP
    lax.fori_loop(0, groups - AHEAD, lambda i, c: (step(i, True), c)[1], 0)
    lax.fori_loop(groups - AHEAD, groups, lambda i, c: (step(i, False), c)[1], 0)
    shipped = packed.at[pl.ds(1, DEVICES - 1)]
    pltpu.make_async_copy(shipped, shipped, all_send).wait()

    def send(src, dst, send_sem, recv_sem, to):
        copy = pltpu.make_async_remote_copy(
            src_ref=src, dst_ref=dst, send_sem=send_sem, recv_sem=recv_sem, device_id=to, device_id_type=MESH
        )
        copy.start()
        return copy

    copies = [
        send(total.at[pl.ds(512, 32)], over_x, over_send.at[0], over_recv.at[0], (xp, gy)),
        send(total.at[pl.ds(MAIN, 64)], over_y, over_send.at[1], over_recv.at[1], (gx, yp)),
        send(total.at[pl.ds(MAIN + 64, 8)], over_c, over_send.at[2], over_recv.at[2], (xp, yp)),
    ]
    for copy in copies:
        copy.wait()
    from_y = jnp.concatenate([over_y[:8] + over_c[...], over_y[8:]], 0)
    inner = total[:512].reshape(64, 8, NZ)
    inner = jnp.concatenate([inner[:4] + over_x[...].reshape(4, 8, NZ), inner[4:]], 0)
    row = lax.broadcasted_iota(jnp.int32, (64, 8, NZ), 1)
    inner = inner + jnp.where(row == 0, from_y[:, None, :], 0.0)
    inner = inner.reshape(WX, 4, 8, NZ)
    porosity = 1.0 / (1.0 + inner[:, 0])
    drag = [inner[:, 1], inner[:, 2], inner[:, 3]]
    porosity_out[...] = porosity
    for m in range(3):
        drag_out[m] = drag[m]

    own_x, own_y = pl.ds(HALO, WX), pl.ds(8, 8)

    def send_halo(k, ref):
        pair = ref[own_x, own_y].reshape(WX // 2, 2, 8, NZ)
        even, odd = pair[:, 0], pair[:, 1]
        upper_half = lax.broadcasted_iota(jnp.int32, (WX // 2, 8, NZ), 1) >= 4
        y_send[k, 0] = jnp.where(upper_half, odd, pltpu.roll(even, 4, 1))
        y_send[k, 1] = jnp.where(upper_half, pltpu.roll(odd, 4, 1), even)
        last = WX // 2 - 1

        def put(i, src, dst, to):
            return send(src, dst, halo_send.at[k, i], halo_recv.at[k, i], to)

        return [
            put(0, y_send.at[k, 0], y_recv.at[k, 0], (gx, yp)),
            put(1, y_send.at[k, 1], y_recv.at[k, 1], (gx, ym)),
            put(2, ref.at[pl.ds(WX, HALO), own_y], ref.at[pl.ds(0, HALO), own_y], (xp, gy)),
            put(3, ref.at[pl.ds(HALO, HALO), own_y], ref.at[pl.ds(WX + HALO, HALO), own_y], (xm, gy)),
            put(4, y_send.at[k, 0, last], corner.at[k, 0], (xp, yp)),
            put(5, y_send.at[k, 1, last], corner.at[k, 1], (xp, ym)),
            put(6, y_send.at[k, 0, 0], corner.at[k, 2], (xm, yp)),
            put(7, y_send.at[k, 1, 0], corner.at[k, 3], (xm, ym)),
        ]

    def place_faces(k, ref):
        low, high = y_recv[k, 0], y_recv[k, 1]
        ref[own_x, :8] = jnp.stack([pltpu.roll(low, 4, 1), low], 1).reshape(WX, 8, NZ)
        ref[own_x, 16:] = jnp.stack([high, pltpu.roll(high, 4, 1)], 1).reshape(WX, 8, NZ)

    def place_corners(k, ref):
        for i, x in ((0, 1), (2, WX + HALO)):
            low, high = corner[k, i], corner[k, i + 1]
            ref[x, :8] = pltpu.roll(low, 4, 0)
            ref[x + 1, :8] = low
            ref[x, 16:] = high
            ref[x + 1, 16:] = pltpu.roll(high, 4, 0)

    poro[own_x, own_y] = porosity
    dx_face[1 : WX + 1] = drag[0]
    dy_send[0] = drag[1][:, 7]
    dy_send[1] = drag[1][:, 0]
    drags = [
        send(dy_send.at[0], dy_recv.at[0], dx_send.at[0], dx_recv.at[0], (gx, yp)),
        send(dy_send.at[1], dy_recv.at[1], dx_send.at[1], dx_recv.at[1], (gx, ym)),
        send(dx_face.at[WX], dx_face.at[0], dx_send.at[2], dx_recv.at[2], (xp, gy)),
        send(dx_face.at[1], dx_face.at[WX + 1], dx_send.at[3], dx_recv.at[3], (xm, gy)),
    ]
    halo = send_halo(0, poro)
    for copy in drags + halo[:4]:
        copy.wait()
    place_faces(0, poro)

    yi = lax.broadcasted_iota(jnp.int32, (WX, 8, NZ), 1)

    def z_next(v):
        return pltpu.roll(v, NZ - 1, 2)

    def z_previous(v):
        return pltpu.roll(v, 1, 2)

    def step_y(v, low, high):
        return jnp.where(yi == 7, high, pltpu.roll(v, 7, 1)), jnp.where(yi == 0, low, pltpu.roll(v, 1, 1))

    after, before = step_y(drag[1], dy_recv[0][:, None, :], dy_recv[1][:, None, :])
    divergence = 0.5 * (dx_face[2:] - dx_face[:WX])
    divergence = divergence + 0.5 * (after - before)
    divergence = divergence + 0.5 * (z_next(drag[2]) - z_previous(drag[2]))
    right_side = source[...] - divergence
    after, before = step_y(porosity, poro[own_x, 7:8], poro[own_x, 16:17])

    def precondition(p, x_after, x_before, y_after, y_before):
        x_upper, x_lower = 0.5 * (p + x_after), 0.5 * (x_before + p)
        y_upper, y_lower = 0.5 * (p + y_after), 0.5 * (y_before + p)
        z_upper = 0.5 * (p + z_next(p))
        z_lower = z_previous(z_upper)
        weights = (x_upper, x_lower, y_upper, y_lower, z_upper, z_lower)
        return weights, 1.0 / (diag_shift + x_upper + x_lower + y_upper + y_lower + z_upper + z_lower)

    start = precondition(
        porosity, poro[pl.ds(HALO + 1, WX), own_y], poro[pl.ds(HALO - 1, WX), own_y], after, before
    )[1] * right_side
    u0[own_x, own_y] = start
    more = send_halo(1, u0)

    for copy in halo[4:]:
        copy.wait()
    place_corners(0, poro)

    def y_steps(v):
        return pltpu.roll(v, 23, 1), pltpu.roll(v, 1, 1)

    p = poro[1 : WIDE - 1]
    weights, precond = precondition(p, poro[2:], poro[: WIDE - 2], *y_steps(p))
    for i, w in enumerate(weights + (precond,)):
        face[i] = w
    for copy in more:
        copy.wait()
    place_faces(1, u0)
    place_corners(1, u0)

    def operate(ref, low):
        high = WIDE - low
        v = ref[low:high]
        w = [face[i, low - 1 : high - 1] for i in range(6)]
        y_after, y_before = y_steps(v)
        result = diag_shift * v
        result = result + w[0] * (v - ref[low + 1 : high + 1])
        result = result + w[1] * (v - ref[low - 1 : high - 1])
        result = result + w[2] * (v - y_after)
        result = result + w[3] * (v - y_before)
        result = result + w[4] * (v - z_next(v))
        return result + w[5] * (v - z_previous(v))

    def partial_sum(a, b):
        product = jnp.sum(a * b, 0)
        return jnp.sum(product[:, :128] + product[:, 128:], 0, keepdims=True)

    a0 = operate(u0, 1)
    u1[1 : WIDE - 1] = face[6] * a0
    a1 = operate(u1, 2)
    u2[2 : WIDE - 2] = face[6, 1 : WX + 3] * a1
    a2 = operate(u2, 3)[:, 8:16]
    a0, a1 = a0[2 : WX + 2, 8:16], a1[1 : WX + 1, 8:16]
    v1, v2 = u1[own_x, own_y], u2[own_x, own_y]
    moments = [
        partial_sum(right_side, start),
        partial_sum(start, a0),
        partial_sum(v1, a0),
        partial_sum(v1, a1),
        partial_sum(v2, a1),
        partial_sum(v2, a2),
    ]

    zero = jnp.zeros((2, 128), f32)
    mine = jnp.concatenate(moments + [zero], 0)
    red[0] = mine
    red_x[gx] = mine
    copies = [
        send(red.at[0], red_x.at[gx], rx_send.at[k], rx_recv.at[k], (lax.rem(gx + k, NGX), gy)) for k in range(1, NGX)
    ]
    for copy in copies:
        copy.wait()
    mine = jnp.sum(red_x[...], 0)
    red[1] = mine
    red_y[gy] = mine
    copies = [
        send(red.at[1], red_y.at[gy], ry_send.at[k], ry_recv.at[k], (gx, lax.rem(gy + k, NGY))) for k in range(1, NGY)
    ]
    for copy in copies:
        copy.wait()
    sums = jnp.sum(jnp.sum(red_y[...], 0), 1, keepdims=True)
    m0, m1, m2, m3, m4, m5 = [sums[i : i + 1] for i in range(6)]
    l21, l31 = m2 / m1, m3 / m1
    d2 = m3 - l21 * m2
    e32 = m4 - l31 * m2
    r1 = m1 - l21 * m0
    r2 = m2 - l31 * m0
    l32 = e32 / d2
    d3 = (m5 - l31 * m3) - l32 * e32
    c2 = (r2 - l32 * r1) / d3
    c1 = r1 / d2 - l32 * c2
    c0 = m0 / m1 - l21 * c1 - l31 * c2
    c0, c1, c2 = [c.reshape(1, 1, 1) for c in (c0, c1, c2)]
    pressure_out[...] = c0 * u0[own_x, own_y] + c1 * u1[own_x, own_y] + c2 * u2[own_x, own_y]


def run(counts, columns, layers, data, source):
    vmem = pl.BlockSpec(memory_space=pltpu.VMEM)
    block = (WX, WY, NZ)
    wide = (WIDE, 24, NZ)
    dma = pltpu.SemaphoreType.DMA
    return pl.pallas_call(
        kernel,
        out_shape=(
            jax.ShapeDtypeStruct(block, f32),
            jax.ShapeDtypeStruct((3,) + block, f32),
            jax.ShapeDtypeStruct(block, f32),
        ),
        in_specs=[pl.BlockSpec(memory_space=pltpu.SMEM), vmem, vmem, vmem, vmem],
        out_specs=(vmem, vmem, vmem),
        scratch_shapes=[
            pltpu.VMEM((DEVICES, 1, VALUES * CAP), f32),
            pltpu.VMEM((DEVICES, 1, VALUES * CAP), f32),
            pltpu.VMEM((ROWS, NZ), f32),
            dma(()), dma((DEVICES // GROUP,)),
            pltpu.VMEM((32, NZ), f32),
            pltpu.VMEM((64, NZ), f32),
            pltpu.VMEM((8, NZ), f32),
            pltpu.VMEM((WX + 2, WY, NZ), f32),
            pltpu.VMEM((2, WX, NZ), f32),
            pltpu.VMEM((2, WX, NZ), f32),
            pltpu.VMEM((2, 2, WX // 2, 8, NZ), f32),
            pltpu.VMEM((2, 2, WX // 2, 8, NZ), f32),
            pltpu.VMEM((2, 4, 8, NZ), f32),
            pltpu.VMEM((7, WIDE - 2, 24, NZ), f32),
            pltpu.VMEM(wide, f32),
            pltpu.VMEM(wide, f32),
            pltpu.VMEM(wide, f32),
            pltpu.VMEM(wide, f32),
            pltpu.VMEM((2, 8, 128), f32),
            pltpu.VMEM((NGX, 8, 128), f32),
            pltpu.VMEM((NGY, 8, 128), f32),
            dma((3,)), dma((3,)), dma((4,)), dma((4,)), dma((2, 8)), dma((2, 8)),
            dma((NGX,)), dma((NGX,)), dma((NGY,)), dma((NGY,)),
        ],
        compiler_params=pltpu.CompilerParams(
            collective_id=0, has_side_effects=True, vmem_limit_bytes=48 << 20
        ),
        name="coupling",
    )(counts, columns, layers, data, source)


def shards(part_column, part_layer, part_count, part_data, source):
    return run(part_count, part_column[0], part_layer[0], part_data[0], source)


def solution(mesh):
    placed = (
        P(("gx", "gy"), None, None),
        P(("gx", "gy"), None, None),
        P(("gx", "gy"), None),
        P(("gx", "gy"), None, None, None),
        P("gx", "gy", None),
    )
    return jax.shard_map(
        shards,
        mesh=mesh,
        in_specs=placed,
        out_specs=(P("gx", "gy", None), P(None, "gx", "gy", None), P("gx", "gy", None)),
        check_vma=False,
    )
```

```python
import jax
import jax.numpy as jnp
from jax import lax
from jax.experimental import pallas as pl
from jax.experimental.pallas import tpu as pltpu
from jax.sharding import PartitionSpec as P

diag_shift = 0.01
WX, WY, NZ, CAP = 16, 8, 256, 256
NGX, NGY = 8, 16
MAIN = (WX + 1) * 4 * WY
ROWS = MAIN + 80
VALUES = 9
f32, bf16 = jnp.float32, jnp.bfloat16
MESH = pl.DeviceIdType.MESH


def tables(slot, k):
    part = [slot[k, :, CAP * i : CAP * (i + 1)] for i in range(VALUES)]
    ox, oy, oz = part[:3]
    column = part[7].astype(jnp.int32)
    bx, by = column >> 3, column & 7
    xi = lax.broadcasted_iota(jnp.int32, (72, CAP), 0) >> 2
    fi = lax.broadcasted_iota(jnp.int32, (8, CAP), 0) & 3
    loads = jnp.where(fi == 0, part[3], jnp.where(fi == 1, part[4], jnp.where(fi == 2, part[5], part[6])))
    wx = jnp.where(bx == xi, 1.0 - ox, jnp.where(bx + 1 == xi, ox, 0.0))
    xf = (wx.reshape(9, 8, CAP) * loads[None]).reshape(72, CAP)
    yi = lax.broadcasted_iota(jnp.int32, (8, CAP), 0)
    wy = jnp.where(by == yi, 1.0 - oy, jnp.where(by + 1 == yi, oy, 0.0))
    over = jnp.where(by == 7, oy, 0.0)
    main = (xf[:68, None, :] * wy[None]).reshape(MAIN, CAP)
    left = jnp.concatenate([main, xf * over, jnp.zeros((8, CAP), f32)], 0)
    high = left.astype(bf16)
    low = (left - high.astype(f32)).astype(bf16)
    q = jnp.round(oz * 256.0) * (1.0 / 256.0)
    e = oz - q
    zi = lax.broadcasted_iota(jnp.int32, (NZ, CAP), 0).astype(f32).astype(bf16)
    here = zi == part[8].astype(bf16)
    above = zi == jnp.where(part[8] == NZ - 1.0, 0.0, part[8] + 1.0).astype(bf16)
    zero = jnp.zeros((), bf16)
    rest = e.astype(bf16)
    z_high = jnp.where(here, (1.0 - q).astype(bf16), jnp.where(above, q.astype(bf16), zero))
    z_low = jnp.where(here, -rest, jnp.where(above, rest, zero))
    return high, low, z_high, z_low


def dot_nt(a, b):
    return lax.dot_general(a, b, (((1,), (1,)), ((), ())), preferred_element_type=f32)


GROUP = 8
HALO = 3
WIDE = WX + 2 * HALO
AHEAD = 4
DEVICES = NGX * NGY


def kernel(
    counts, columns, layers, data, source, porosity_out, drag_out, pressure_out,
    packed, slots, total, ready, all_send, all_recv,
    over_x, over_y, over_c, dx_face, dy_send, dy_recv, y_send, y_recv, corner, face, poro, u0, u1, u2,
    red, red_x, red_y, over_send, over_recv, dx_send, dx_recv, halo_send, halo_recv, rx_send, rx_recv, ry_send, ry_recv,
):
    gx, gy = lax.axis_index("gx"), lax.axis_index("gy")
    xp, xm = lax.rem(gx + 1, NGX), lax.rem(gx + NGX - 1, NGX)
    yp, ym = lax.rem(gy + 1, NGY), lax.rem(gy + NGY - 1, NGY)

    near = NGX + NGY - 1

    def peer(k):
        if isinstance(k, int) and k < near:
            step_x, step_y = (k, 0) if k < NGX else (0, k - NGX + 1)
        else:
            step_x, step_y = 1 + lax.rem(k - near, NGX - 1), 1 + lax.div(k - near, NGX - 1)
        return lax.rem(gx + step_x, NGX), lax.rem(gy + step_y, NGY)

    barrier = pltpu.get_barrier_semaphore()
    for k in range(1, near):
        pl.semaphore_signal(barrier, inc=1, device_id=peer(k), device_id_type=MESH)

    lane = lax.broadcasted_iota(jnp.int32, (1, CAP), 1)

    def pack(target, k, d):
        live = lane < counts[0, d]
        rows = data[d]
        for i in range(7):
            row = rows[i : i + 1]
            target[k, :, CAP * i : CAP * (i + 1)] = row if i < 3 else jnp.where(live, row, 0.0)
        target[k, :, CAP * 7 : CAP * 8] = columns[pl.ds(d, 1)].astype(f32)
        target[k, :, CAP * 8 :] = layers[pl.ds(d, 1)].astype(f32)

    def pack_one(k):
        px, py = peer(k)
        pack(packed, k, px * NGY + py)

    for k in range(1, near):
        pack_one(k)
    pack(slots, 0, gx * NGY + gy)

    def ship(group, g):
        k = group * GROUP + g
        pltpu.make_async_remote_copy(
            src_ref=packed.at[k],
            dst_ref=slots.at[k],
            send_sem=all_send,
            recv_sem=all_recv.at[group],
            device_id=peer(k),
            device_id_type=MESH,
        ).start()

    pl.semaphore_wait(barrier, near - 1)
    for k in range(1, NGY):
        pl.semaphore_signal(ready, inc=1, device_id=(gx, lax.rem(gy + k, NGY)), device_id_type=MESH)
    for k in range(1, near):
        ship(k // GROUP, k % GROUP)
    for k in range(near, AHEAD * GROUP):
        pack_one(k)
    pl.semaphore_wait(ready, NGY - 1)
    for k in range(near, AHEAD * GROUP):
        ship(k // GROUP, k % GROUP)

    def arrived(group, first, count):
        block = slots.at[pl.ds(first, count)]
        pltpu.make_async_copy(block, block, all_recv.at[group]).wait()

    def add_group(i):
        left, right = [], []
        for g in range(GROUP):
            high, low, z_high, z_low = tables(slots, i * GROUP + g)
            left += [high, low, high]
            right += [z_high, z_high, z_low]
        return dot_nt(jnp.concatenate(left, 1), jnp.concatenate(right, 1))

    total[...] = jnp.zeros_like(total)

    def step(i, shipping):
        @pl.when(i == 0)
        def _():
            arrived(0, 1, GROUP - 1)

        @pl.when(i > 0)
        def _():
            arrived(i, i * GROUP, GROUP)

        if shipping:
            for g in range(GROUP):
                pack_one((i + AHEAD) * GROUP + g)
                ship(i + AHEAD, g)
        total[...] += add_group(i)

    groups = DEVICES // GROUP
    lax.fori_loop(0, groups - AHEAD, lambda i, c: (step(i, True), c)[1], 0)
    lax.fori_loop(groups - AHEAD, groups, lambda i, c: (step(i, False), c)[1], 0)
    shipped = packed.at[pl.ds(1, DEVICES - 1)]
    pltpu.make_async_copy(shipped, shipped, all_send).wait()

    def send(src, dst, send_sem, recv_sem, to):
        copy = pltpu.make_async_remote_copy(
            src_ref=src, dst_ref=dst, send_sem=send_sem, recv_sem=recv_sem, device_id=to, device_id_type=MESH
        )
        copy.start()
        return copy

    copies = [
        send(total.at[pl.ds(512, 32)], over_x, over_send.at[0], over_recv.at[0], (xp, gy)),
        send(total.at[pl.ds(MAIN, 64)], over_y, over_send.at[1], over_recv.at[1], (gx, yp)),
        send(total.at[pl.ds(MAIN + 64, 8)], over_c, over_send.at[2], over_recv.at[2], (xp, yp)),
    ]
    for copy in copies:
        copy.wait()
    from_y = jnp.concatenate([over_y[:8] + over_c[...], over_y[8:]], 0)
    inner = total[:512].reshape(64, 8, NZ)
    inner = jnp.concatenate([inner[:4] + over_x[...].reshape(4, 8, NZ), inner[4:]], 0)
    row = lax.broadcasted_iota(jnp.int32, (64, 8, NZ), 1)
    inner = inner + jnp.where(row == 0, from_y[:, None, :], 0.0)
    inner = inner.reshape(WX, 4, 8, NZ)
    porosity = 1.0 / (1.0 + inner[:, 0])
    drag = [inner[:, 1], inner[:, 2], inner[:, 3]]
    porosity_out[...] = porosity
    for m in range(3):
        drag_out[m] = drag[m]

    own_x, own_y = pl.ds(HALO, WX), pl.ds(8, 8)

    def send_halo(k, ref):
        pair = ref[own_x, own_y].reshape(WX // 2, 2, 8, NZ)
        even, odd = pair[:, 0], pair[:, 1]
        upper_half = lax.broadcasted_iota(jnp.int32, (WX // 2, 8, NZ), 1) >= 4
        y_send[k, 0] = jnp.where(upper_half, odd, pltpu.roll(even, 4, 1))
        y_send[k, 1] = jnp.where(upper_half, pltpu.roll(odd, 4, 1), even)
        last = WX // 2 - 1

        def put(i, src, dst, to):
            return send(src, dst, halo_send.at[k, i], halo_recv.at[k, i], to)

        return [
            put(0, y_send.at[k, 0], y_recv.at[k, 0], (gx, yp)),
            put(1, y_send.at[k, 1], y_recv.at[k, 1], (gx, ym)),
            put(2, ref.at[pl.ds(WX, HALO), own_y], ref.at[pl.ds(0, HALO), own_y], (xp, gy)),
            put(3, ref.at[pl.ds(HALO, HALO), own_y], ref.at[pl.ds(WX + HALO, HALO), own_y], (xm, gy)),
            put(4, y_send.at[k, 0, last], corner.at[k, 0], (xp, yp)),
            put(5, y_send.at[k, 1, last], corner.at[k, 1], (xp, ym)),
            put(6, y_send.at[k, 0, 0], corner.at[k, 2], (xm, yp)),
            put(7, y_send.at[k, 1, 0], corner.at[k, 3], (xm, ym)),
        ]

    def place_faces(k, ref):
        low, high = y_recv[k, 0], y_recv[k, 1]
        ref[own_x, :8] = jnp.stack([pltpu.roll(low, 4, 1), low], 1).reshape(WX, 8, NZ)
        ref[own_x, 16:] = jnp.stack([high, pltpu.roll(high, 4, 1)], 1).reshape(WX, 8, NZ)

    def place_corners(k, ref):
        for i, x in ((0, 1), (2, WX + HALO)):
            low, high = corner[k, i], corner[k, i + 1]
            ref[x, :8] = pltpu.roll(low, 4, 0)
            ref[x + 1, :8] = low
            ref[x, 16:] = high
            ref[x + 1, 16:] = pltpu.roll(high, 4, 0)

    poro[own_x, own_y] = porosity
    dx_face[1 : WX + 1] = drag[0]
    dy_send[0] = drag[1][:, 7]
    dy_send[1] = drag[1][:, 0]
    drags = [
        send(dy_send.at[0], dy_recv.at[0], dx_send.at[0], dx_recv.at[0], (gx, yp)),
        send(dy_send.at[1], dy_recv.at[1], dx_send.at[1], dx_recv.at[1], (gx, ym)),
        send(dx_face.at[WX], dx_face.at[0], dx_send.at[2], dx_recv.at[2], (xp, gy)),
        send(dx_face.at[1], dx_face.at[WX + 1], dx_send.at[3], dx_recv.at[3], (xm, gy)),
    ]
    halo = send_halo(0, poro)
    for copy in drags + halo[:4]:
        copy.wait()
    place_faces(0, poro)

    yi = lax.broadcasted_iota(jnp.int32, (WX, 8, NZ), 1)

    def z_next(v):
        return pltpu.roll(v, NZ - 1, 2)

    def z_previous(v):
        return pltpu.roll(v, 1, 2)

    def step_y(v, low, high):
        return jnp.where(yi == 7, high, pltpu.roll(v, 7, 1)), jnp.where(yi == 0, low, pltpu.roll(v, 1, 1))

    after, before = step_y(drag[1], dy_recv[0][:, None, :], dy_recv[1][:, None, :])
    divergence = 0.5 * (dx_face[2:] - dx_face[:WX])
    divergence = divergence + 0.5 * (after - before)
    divergence = divergence + 0.5 * (z_next(drag[2]) - z_previous(drag[2]))
    right_side = source[...] - divergence
    after, before = step_y(porosity, poro[own_x, 7:8], poro[own_x, 16:17])

    def precondition(p, x_after, x_before, y_after, y_before):
        x_upper, x_lower = 0.5 * (p + x_after), 0.5 * (x_before + p)
        y_upper, y_lower = 0.5 * (p + y_after), 0.5 * (y_before + p)
        z_upper = 0.5 * (p + z_next(p))
        z_lower = z_previous(z_upper)
        weights = (x_upper, x_lower, y_upper, y_lower, z_upper, z_lower)
        return weights, 1.0 / (diag_shift + x_upper + x_lower + y_upper + y_lower + z_upper + z_lower)

    start = precondition(
        porosity, poro[pl.ds(HALO + 1, WX), own_y], poro[pl.ds(HALO - 1, WX), own_y], after, before
    )[1] * right_side
    u0[own_x, own_y] = start
    more = send_halo(1, u0)

    for copy in halo[4:]:
        copy.wait()
    place_corners(0, poro)

    def y_steps(v):
        return pltpu.roll(v, 23, 1), pltpu.roll(v, 1, 1)

    p = poro[1 : WIDE - 1]
    weights, precond = precondition(p, poro[2:], poro[: WIDE - 2], *y_steps(p))
    for i, w in enumerate(weights + (precond,)):
        face[i] = w
    for copy in more:
        copy.wait()
    place_faces(1, u0)
    place_corners(1, u0)

    def operate(ref, low):
        high = WIDE - low
        v = ref[low:high]
        w = [face[i, low - 1 : high - 1] for i in range(6)]
        y_after, y_before = y_steps(v)
        result = diag_shift * v
        result = result + w[0] * (v - ref[low + 1 : high + 1])
        result = result + w[1] * (v - ref[low - 1 : high - 1])
        result = result + w[2] * (v - y_after)
        result = result + w[3] * (v - y_before)
        result = result + w[4] * (v - z_next(v))
        return result + w[5] * (v - z_previous(v))

    def partial_sum(a, b):
        product = jnp.sum(a * b, 0)
        return jnp.sum(product[:, :128] + product[:, 128:], 0, keepdims=True)

    a0 = operate(u0, 1)
    u1[1 : WIDE - 1] = face[6] * a0
    a1 = operate(u1, 2)
    u2[2 : WIDE - 2] = face[6, 1 : WX + 3] * a1
    a2 = operate(u2, 3)[:, 8:16]
    a0, a1 = a0[2 : WX + 2, 8:16], a1[1 : WX + 1, 8:16]
    v1, v2 = u1[own_x, own_y], u2[own_x, own_y]
    moments = [
        partial_sum(right_side, start),
        partial_sum(start, a0),
        partial_sum(v1, a0),
        partial_sum(v1, a1),
        partial_sum(v2, a1),
        partial_sum(v2, a2),
    ]

    zero = jnp.zeros((2, 128), f32)
    mine = jnp.concatenate(moments + [zero], 0)
    red[0] = mine
    red_x[gx] = mine
    copies = [
        send(red.at[0], red_x.at[gx], rx_send.at[k], rx_recv.at[k], (lax.rem(gx + k, NGX), gy)) for k in range(1, NGX)
    ]
    for copy in copies:
        copy.wait()
    mine = jnp.sum(red_x[...], 0)
    red[1] = mine
    red_y[gy] = mine
    copies = [
        send(red.at[1], red_y.at[gy], ry_send.at[k], ry_recv.at[k], (gx, lax.rem(gy + k, NGY))) for k in range(1, NGY)
    ]
    for copy in copies:
        copy.wait()
    sums = jnp.sum(jnp.sum(red_y[...], 0), 1, keepdims=True)
    m0, m1, m2, m3, m4, m5 = [sums[i : i + 1] for i in range(6)]
    l21, l31 = m2 / m1, m3 / m1
    d2 = m3 - l21 * m2
    e32 = m4 - l31 * m2
    r1 = m1 - l21 * m0
    r2 = m2 - l31 * m0
    l32 = jnp.where(d2 > 1e-8 * m3, e32 / d2, 0.0)
    d3 = (m5 - l31 * m3) - l32 * e32
    c2 = jnp.where(d3 > 1e-8 * m5, (r2 - l32 * r1) / d3, 0.0)
    c1 = jnp.where(d2 > 1e-8 * m3, r1 / d2 - l32 * c2, 0.0)
    c0 = m0 / m1 - l21 * c1 - l31 * c2
    c0, c1, c2 = [c.reshape(1, 1, 1) for c in (c0, c1, c2)]
    pressure_out[...] = c0 * u0[own_x, own_y] + c1 * u1[own_x, own_y] + c2 * u2[own_x, own_y]


def run(counts, columns, layers, data, source):
    vmem = pl.BlockSpec(memory_space=pltpu.VMEM)
    block = (WX, WY, NZ)
    wide = (WIDE, 24, NZ)
    dma = pltpu.SemaphoreType.DMA
    return pl.pallas_call(
        kernel,
        out_shape=(
            jax.ShapeDtypeStruct(block, f32),
            jax.ShapeDtypeStruct((3,) + block, f32),
            jax.ShapeDtypeStruct(block, f32),
        ),
        in_specs=[pl.BlockSpec(memory_space=pltpu.SMEM), vmem, vmem, vmem, vmem],
        out_specs=(vmem, vmem, vmem),
        scratch_shapes=[
            pltpu.VMEM((DEVICES, 1, VALUES * CAP), f32),
            pltpu.VMEM((DEVICES, 1, VALUES * CAP), f32),
            pltpu.VMEM((ROWS, NZ), f32),
            pltpu.SemaphoreType.REGULAR, dma(()), dma((DEVICES // GROUP,)),
            pltpu.VMEM((32, NZ), f32),
            pltpu.VMEM((64, NZ), f32),
            pltpu.VMEM((8, NZ), f32),
            pltpu.VMEM((WX + 2, WY, NZ), f32),
            pltpu.VMEM((2, WX, NZ), f32),
            pltpu.VMEM((2, WX, NZ), f32),
            pltpu.VMEM((2, 2, WX // 2, 8, NZ), f32),
            pltpu.VMEM((2, 2, WX // 2, 8, NZ), f32),
            pltpu.VMEM((2, 4, 8, NZ), f32),
            pltpu.VMEM((7, WIDE - 2, 24, NZ), f32),
            pltpu.VMEM(wide, f32),
            pltpu.VMEM(wide, f32),
            pltpu.VMEM(wide, f32),
            pltpu.VMEM(wide, f32),
            pltpu.VMEM((2, 8, 128), f32),
            pltpu.VMEM((NGX, 8, 128), f32),
            pltpu.VMEM((NGY, 8, 128), f32),
            dma((3,)), dma((3,)), dma((4,)), dma((4,)), dma((2, 8)), dma((2, 8)),
            dma((NGX,)), dma((NGX,)), dma((NGY,)), dma((NGY,)),
        ],
        compiler_params=pltpu.CompilerParams(
            collective_id=0, has_side_effects=True, vmem_limit_bytes=48 << 20
        ),
        name="coupling",
    )(counts, columns, layers, data, source)


def shards(part_column, part_layer, part_count, part_data, source):
    return run(part_count, part_column[0], part_layer[0], part_data[0], source)


def solution(mesh):
    placed = (
        P(("gx", "gy"), None, None),
        P(("gx", "gy"), None, None),
        P(("gx", "gy"), None),
        P(("gx", "gy"), None, None, None),
        P("gx", "gy", None),
    )
    return jax.shard_map(
        shards,
        mesh=mesh,
        in_specs=placed,
        out_specs=(P("gx", "gy", None), P(None, "gx", "gy", None), P("gx", "gy", None)),
        check_vma=False,
    )
```

```python
import jax
import jax.numpy as jnp
from jax import lax
from jax.experimental import pallas as pl
from jax.experimental.pallas import tpu as pltpu
from jax.sharding import PartitionSpec as P

diag_shift = 0.01
WX, WY, NZ, CAP = 16, 8, 256, 256
NGX, NGY = 8, 16
MAIN = (WX + 1) * 4 * WY
ROWS = MAIN + 80
VALUES = 9
f32, bf16 = jnp.float32, jnp.bfloat16
MESH = pl.DeviceIdType.MESH


def tables(slot, k):
    part = [slot[k, :, CAP * i : CAP * (i + 1)] for i in range(VALUES)]
    ox, oy, oz = part[:3]
    column = part[7].astype(jnp.int32)
    bx, by = column >> 3, column & 7
    xi = lax.broadcasted_iota(jnp.int32, (72, CAP), 0) >> 2
    fi = lax.broadcasted_iota(jnp.int32, (8, CAP), 0) & 3
    loads = jnp.where(fi == 0, part[3], jnp.where(fi == 1, part[4], jnp.where(fi == 2, part[5], part[6])))
    wx = jnp.where(bx == xi, 1.0 - ox, jnp.where(bx + 1 == xi, ox, 0.0))
    xf = (wx.reshape(9, 8, CAP) * loads[None]).reshape(72, CAP)
    yi = lax.broadcasted_iota(jnp.int32, (8, CAP), 0)
    wy = jnp.where(by == yi, 1.0 - oy, jnp.where(by + 1 == yi, oy, 0.0))
    over = jnp.where(by == 7, oy, 0.0)
    main = (xf[:68, None, :] * wy[None]).reshape(MAIN, CAP)
    left = jnp.concatenate([main, xf * over, jnp.zeros((8, CAP), f32)], 0)
    high = left.astype(bf16)
    low = (left - high.astype(f32)).astype(bf16)
    q = jnp.round(oz * 256.0) * (1.0 / 256.0)
    e = oz - q
    zi = lax.broadcasted_iota(jnp.int32, (NZ, CAP), 0).astype(f32).astype(bf16)
    here = zi == part[8].astype(bf16)
    above = zi == jnp.where(part[8] == NZ - 1.0, 0.0, part[8] + 1.0).astype(bf16)
    zero = jnp.zeros((), bf16)
    rest = e.astype(bf16)
    z_high = jnp.where(here, (1.0 - q).astype(bf16), jnp.where(above, q.astype(bf16), zero))
    z_low = jnp.where(here, -rest, jnp.where(above, rest, zero))
    return high, low, z_high, z_low


def dot_nt(a, b):
    return lax.dot_general(a, b, (((1,), (1,)), ((), ())), preferred_element_type=f32)


GROUP = 8
HALO = 3
WIDE = WX + 2 * HALO
AHEAD = 4
DEVICES = NGX * NGY


def kernel(
    counts, columns, layers, data, source, porosity_out, drag_out, pressure_out,
    packed, slots, total, ready, all_send, all_recv,
    over_x, over_y, over_c, next_x, diag_y, diag_x, cross_y, cross_x, tip, f_send, f_recv, y_send, y_recv, corner, face, poro, u0, u1, u2,
    red, red_x, red_y, edge_send, edge_recv, halo_send, halo_recv, rx_send, rx_recv, ry_send, ry_recv,
):
    gx, gy = lax.axis_index("gx"), lax.axis_index("gy")
    xp, xm = lax.rem(gx + 1, NGX), lax.rem(gx + NGX - 1, NGX)
    yp, ym = lax.rem(gy + 1, NGY), lax.rem(gy + NGY - 1, NGY)

    near = NGX + NGY - 1

    def peer(k):
        if isinstance(k, int) and k < near:
            step_x, step_y = (k, 0) if k < NGX else (0, k - NGX + 1)
        else:
            step_x, step_y = 1 + lax.rem(k - near, NGX - 1), 1 + lax.div(k - near, NGX - 1)
        return lax.rem(gx + step_x, NGX), lax.rem(gy + step_y, NGY)

    barrier = pltpu.get_barrier_semaphore()
    for k in range(1, near):
        pl.semaphore_signal(barrier, inc=1, device_id=peer(k), device_id_type=MESH)

    lane = lax.broadcasted_iota(jnp.int32, (1, CAP), 1)

    def pack(target, k, d):
        live = lane < counts[0, d]
        rows = data[d]
        for i in range(7):
            row = rows[i : i + 1]
            target[k, :, CAP * i : CAP * (i + 1)] = row if i < 3 else jnp.where(live, row, 0.0)
        target[k, :, CAP * 7 : CAP * 8] = columns[pl.ds(d, 1)].astype(f32)
        target[k, :, CAP * 8 :] = layers[pl.ds(d, 1)].astype(f32)

    def pack_one(k):
        px, py = peer(k)
        pack(packed, k, px * NGY + py)

    for k in range(1, near):
        pack_one(k)
    pack(slots, 0, gx * NGY + gy)

    def ship(group, g):
        k = group * GROUP + g
        pltpu.make_async_remote_copy(
            src_ref=packed.at[k],
            dst_ref=slots.at[k],
            send_sem=all_send,
            recv_sem=all_recv.at[group],
            device_id=peer(k),
            device_id_type=MESH,
        ).start()

    pl.semaphore_wait(barrier, near - 1)
    for k in range(1, NGY):
        pl.semaphore_signal(ready, inc=1, device_id=(gx, lax.rem(gy + k, NGY)), device_id_type=MESH)
    for k in range(1, near):
        ship(k // GROUP, k % GROUP)
    for k in range(near, AHEAD * GROUP):
        pack_one(k)
    pl.semaphore_wait(ready, NGY - 1)
    for k in range(near, AHEAD * GROUP):
        ship(k // GROUP, k % GROUP)

    def arrived(group, first, count):
        block = slots.at[pl.ds(first, count)]
        pltpu.make_async_copy(block, block, all_recv.at[group]).wait()

    def add_group(i):
        left, right = [], []
        for g in range(GROUP):
            high, low, z_high, z_low = tables(slots, i * GROUP + g)
            left += [high, low, high]
            right += [z_high, z_high, z_low]
        return dot_nt(jnp.concatenate(left, 1), jnp.concatenate(right, 1))

    total[...] = jnp.zeros_like(total)

    def step(i, shipping):
        @pl.when(i == 0)
        def _():
            arrived(0, 1, GROUP - 1)

        @pl.when(i > 0)
        def _():
            arrived(i, i * GROUP, GROUP)

        if shipping:
            for g in range(GROUP):
                pack_one((i + AHEAD) * GROUP + g)
                ship(i + AHEAD, g)
        total[...] += add_group(i)

    groups = DEVICES // GROUP
    lax.fori_loop(0, groups - AHEAD, lambda i, c: (step(i, True), c)[1], 0)
    lax.fori_loop(groups - AHEAD, groups, lambda i, c: (step(i, False), c)[1], 0)
    shipped = packed.at[pl.ds(1, DEVICES - 1)]
    pltpu.make_async_copy(shipped, shipped, all_send).wait()

    def send(src, dst, send_sem, recv_sem, to):
        copy = pltpu.make_async_remote_copy(
            src_ref=src, dst_ref=dst, send_sem=send_sem, recv_sem=recv_sem, device_id=to, device_id_type=MESH
        )
        copy.start()
        return copy

    top, side = 4 * WX * WY, 4 * WX
    ends = total[top:MAIN].reshape(4, 8, NZ)
    tip[...] = jnp.concatenate([ends[:, 7], ends[:, 0]], 0)
    blocks = total[:top].reshape(WX, 4, 8, NZ)
    for i, y in enumerate((7, 0)):
        f_send[i, 0] = blocks[:, 0, y]
        f_send[i, 1] = blocks[:, 2, y]
    routes = [
        (total.at[pl.ds(MAIN + side - 8, 16)], diag_y, (xp, yp)),
        (tip, diag_x, (xp, yp)),
        (total.at[pl.ds(MAIN, 8)], cross_y, (xm, yp)),
        (tip, cross_x, (xp, ym)),
        (total.at[pl.ds(MAIN, side + 8)], over_y, (gx, yp)),
        (f_send.at[0], f_recv.at[0], (gx, yp)),
        (f_send.at[1], f_recv.at[1], (gx, ym)),
        (total.at[pl.ds(top - 32, 64)], over_x, (xp, gy)),
        (total.at[pl.ds(MAIN + side, 8)], over_c, (xp, gy)),
        (total.at[pl.ds(0, 16)], next_x, (xm, gy)),
    ]
    edges = [send(src, dst, edge_send.at[i], edge_recv.at[i], to) for i, (src, dst, to) in enumerate(routes)]
    for copy in edges:
        copy.wait()

    from_y = jnp.concatenate([over_y[:8] + diag_y[8:], over_y[8:side]], 0)
    inner = total[:top].reshape(side, 8, NZ)
    inner = jnp.concatenate([inner[:4] + over_x[32:].reshape(4, 8, NZ), inner[4:]], 0)
    row = lax.broadcasted_iota(jnp.int32, (side, 8, NZ), 1)
    inner = inner + jnp.where(row == 0, from_y[:, None, :], 0.0)
    inner = inner.reshape(WX, 4, 8, NZ)
    porosity = 1.0 / (1.0 + inner[:, 0])
    drag = [inner[:, 1], inner[:, 2], inner[:, 3]]
    porosity_out[...] = porosity
    for m in range(3):
        drag_out[m] = drag[m]

    own_x, own_y = pl.ds(HALO, WX), pl.ds(8, 8)

    def send_halo(k, ref):
        pair = ref[own_x, own_y].reshape(WX // 2, 2, 8, NZ)
        even, odd = pair[:, 0], pair[:, 1]
        upper_half = lax.broadcasted_iota(jnp.int32, (WX // 2, 8, NZ), 1) >= 4
        y_send[k, 0] = jnp.where(upper_half, odd, pltpu.roll(even, 4, 1))
        y_send[k, 1] = jnp.where(upper_half, pltpu.roll(odd, 4, 1), even)
        last = WX // 2 - 1

        def put(i, src, dst, to):
            return send(src, dst, halo_send.at[k, i], halo_recv.at[k, i], to)

        return [
            put(0, y_send.at[k, 0, last], corner.at[k, 0], (xp, yp)),
            put(1, y_send.at[k, 1, last], corner.at[k, 1], (xp, ym)),
            put(2, y_send.at[k, 0, 0], corner.at[k, 2], (xm, yp)),
            put(3, y_send.at[k, 1, 0], corner.at[k, 3], (xm, ym)),
            put(4, y_send.at[k, 0], y_recv.at[k, 0], (gx, yp)),
            put(5, y_send.at[k, 1], y_recv.at[k, 1], (gx, ym)),
            put(6, ref.at[pl.ds(WX, HALO), own_y], ref.at[pl.ds(0, HALO), own_y], (xp, gy)),
            put(7, ref.at[pl.ds(HALO, HALO), own_y], ref.at[pl.ds(WX + HALO, HALO), own_y], (xm, gy)),
        ]

    def place_faces(k, ref):
        low, high = y_recv[k, 0], y_recv[k, 1]
        ref[own_x, :8] = jnp.stack([pltpu.roll(low, 4, 1), low], 1).reshape(WX, 8, NZ)
        ref[own_x, 16:] = jnp.stack([high, pltpu.roll(high, 4, 1)], 1).reshape(WX, 8, NZ)

    def place_corners(k, ref):
        for i, x in ((0, 1), (2, WX + HALO)):
            low, high = corner[k, i], corner[k, i + 1]
            ref[x, :8] = pltpu.roll(low, 4, 0)
            ref[x + 1, :8] = low
            ref[x, 16:] = high
            ref[x + 1, 16:] = pltpu.roll(high, 4, 0)

    poro[own_x, own_y] = porosity
    halo = send_halo(0, poro)

    first_y = lax.broadcasted_iota(jnp.int32, (2, 8, NZ), 1) == 0
    below_x = over_x[:16].reshape(2, 8, NZ) + jnp.where(first_y, diag_y[4:6][:, None, :], 0.0)
    above_x = next_x[...].reshape(2, 8, NZ) + total[top : top + 16].reshape(2, 8, NZ)
    above_x = above_x + jnp.where(first_y, (cross_y[:2] + over_y[side : side + 2])[:, None, :], 0.0)
    first_x = lax.broadcasted_iota(jnp.int32, (WX, NZ), 0) == 0
    mine = total[MAIN : MAIN + side].reshape(WX, 4, NZ)
    below_y, above_y = [], []
    for i, f in enumerate((0, 2)):
        below_y.append(f_recv[0, i] + jnp.where(first_x, diag_x[f : f + 1], 0.0))
        corner_sum = cross_x[4 + f : 5 + f] + over_c[f : f + 1]
        above_y.append(f_recv[1, i] + mine[:, f] + jnp.where(first_x, corner_sum, 0.0))

    yi = lax.broadcasted_iota(jnp.int32, (WX, 8, NZ), 1)

    def z_next(v):
        return pltpu.roll(v, NZ - 1, 2)

    def z_previous(v):
        return pltpu.roll(v, 1, 2)

    def step_y(v, low, high):
        return jnp.where(yi == 7, high, pltpu.roll(v, 7, 1)), jnp.where(yi == 0, low, pltpu.roll(v, 1, 1))

    def step_x(v, low, high):
        return jnp.concatenate([v[1:], high[None]], 0), jnp.concatenate([low[None], v[: WX - 1]], 0)

    after, before = step_y(drag[1], below_y[1][:, None, :], above_y[1][:, None, :])
    x_after, x_before = step_x(drag[0], below_x[1], above_x[1])
    divergence = 0.5 * (x_after - x_before)
    divergence = divergence + 0.5 * (after - before)
    divergence = divergence + 0.5 * (z_next(drag[2]) - z_previous(drag[2]))
    right_side = source[...] - divergence
    low, high = 1.0 / (1.0 + below_y[0]), 1.0 / (1.0 + above_y[0])
    after, before = step_y(porosity, low[:, None, :], high[:, None, :])
    x_after, x_before = step_x(porosity, 1.0 / (1.0 + below_x[0]), 1.0 / (1.0 + above_x[0]))

    def precondition(p, x_after, x_before, y_after, y_before):
        x_upper, x_lower = 0.5 * (p + x_after), 0.5 * (x_before + p)
        y_upper, y_lower = 0.5 * (p + y_after), 0.5 * (y_before + p)
        z_upper = 0.5 * (p + z_next(p))
        z_lower = z_previous(z_upper)
        weights = (x_upper, x_lower, y_upper, y_lower, z_upper, z_lower)
        return weights, 1.0 / (diag_shift + x_upper + x_lower + y_upper + y_lower + z_upper + z_lower)

    start = precondition(porosity, x_after, x_before, after, before)[1] * right_side
    u0[own_x, own_y] = start
    more = send_halo(1, u0)

    for copy in halo:
        copy.wait()
    place_faces(0, poro)
    place_corners(0, poro)

    def y_steps(v):
        return pltpu.roll(v, 23, 1), pltpu.roll(v, 1, 1)

    p = poro[1 : WIDE - 1]
    weights, precond = precondition(p, poro[2:], poro[: WIDE - 2], *y_steps(p))
    for i, w in enumerate(weights + (precond,)):
        face[i] = w
    for copy in more:
        copy.wait()
    place_faces(1, u0)
    place_corners(1, u0)

    def operate(ref, low):
        high = WIDE - low
        v = ref[low:high]
        w = [face[i, low - 1 : high - 1] for i in range(6)]
        y_after, y_before = y_steps(v)
        result = diag_shift * v
        result = result + w[0] * (v - ref[low + 1 : high + 1])
        result = result + w[1] * (v - ref[low - 1 : high - 1])
        result = result + w[2] * (v - y_after)
        result = result + w[3] * (v - y_before)
        result = result + w[4] * (v - z_next(v))
        return result + w[5] * (v - z_previous(v))

    def partial_sum(a, b):
        product = jnp.sum(a * b, 0)
        return jnp.sum(product[:, :128] + product[:, 128:], 0, keepdims=True)

    a0 = operate(u0, 1)
    u1[1 : WIDE - 1] = face[6] * a0
    a1 = operate(u1, 2)
    u2[2 : WIDE - 2] = face[6, 1 : WX + 3] * a1
    a2 = operate(u2, 3)[:, 8:16]
    a0, a1 = a0[2 : WX + 2, 8:16], a1[1 : WX + 1, 8:16]
    v1, v2 = u1[own_x, own_y], u2[own_x, own_y]
    moments = [
        partial_sum(right_side, start),
        partial_sum(start, a0),
        partial_sum(v1, a0),
        partial_sum(v1, a1),
        partial_sum(v2, a1),
        partial_sum(v2, a2),
    ]

    zero = jnp.zeros((2, 128), f32)
    mine = jnp.concatenate(moments + [zero], 0)
    red[0] = mine
    red_x[gx] = mine
    copies = [
        send(red.at[0], red_x.at[gx], rx_send.at[k], rx_recv.at[k], (lax.rem(gx + k, NGX), gy)) for k in range(1, NGX)
    ]
    for copy in copies:
        copy.wait()
    mine = jnp.sum(red_x[...], 0)
    red[1] = mine
    red_y[gy] = mine
    copies = [
        send(red.at[1], red_y.at[gy], ry_send.at[k], ry_recv.at[k], (gx, lax.rem(gy + k, NGY))) for k in range(1, NGY)
    ]
    for copy in copies:
        copy.wait()
    sums = jnp.sum(jnp.sum(red_y[...], 0), 1, keepdims=True)
    m0, m1, m2, m3, m4, m5 = [sums[i : i + 1] for i in range(6)]
    l21, l31 = m2 / m1, m3 / m1
    d2 = m3 - l21 * m2
    e32 = m4 - l31 * m2
    r1 = m1 - l21 * m0
    r2 = m2 - l31 * m0
    l32 = jnp.where(d2 > 1e-8 * m3, e32 / d2, 0.0)
    d3 = (m5 - l31 * m3) - l32 * e32
    c2 = jnp.where(d3 > 1e-8 * m5, (r2 - l32 * r1) / d3, 0.0)
    c1 = jnp.where(d2 > 1e-8 * m3, r1 / d2 - l32 * c2, 0.0)
    c0 = m0 / m1 - l21 * c1 - l31 * c2
    c0, c1, c2 = [c.reshape(1, 1, 1) for c in (c0, c1, c2)]
    pressure_out[...] = c0 * u0[own_x, own_y] + c1 * u1[own_x, own_y] + c2 * u2[own_x, own_y]


def run(counts, columns, layers, data, source):
    vmem = pl.BlockSpec(memory_space=pltpu.VMEM)
    block = (WX, WY, NZ)
    wide = (WIDE, 24, NZ)
    dma = pltpu.SemaphoreType.DMA
    return pl.pallas_call(
        kernel,
        out_shape=(
            jax.ShapeDtypeStruct(block, f32),
            jax.ShapeDtypeStruct((3,) + block, f32),
            jax.ShapeDtypeStruct(block, f32),
        ),
        in_specs=[pl.BlockSpec(memory_space=pltpu.SMEM), vmem, vmem, vmem, vmem],
        out_specs=(vmem, vmem, vmem),
        scratch_shapes=[
            pltpu.VMEM((DEVICES, 1, VALUES * CAP), f32),
            pltpu.VMEM((DEVICES, 1, VALUES * CAP), f32),
            pltpu.VMEM((ROWS, NZ), f32),
            pltpu.SemaphoreType.REGULAR, dma(()), dma((DEVICES // GROUP,)),
            pltpu.VMEM((64, NZ), f32),
            pltpu.VMEM((72, NZ), f32),
            pltpu.VMEM((8, NZ), f32),
            pltpu.VMEM((16, NZ), f32),
            pltpu.VMEM((16, NZ), f32),
            pltpu.VMEM((8, NZ), f32),
            pltpu.VMEM((8, NZ), f32),
            pltpu.VMEM((8, NZ), f32),
            pltpu.VMEM((8, NZ), f32),
            pltpu.VMEM((2, 2, WX, NZ), f32),
            pltpu.VMEM((2, 2, WX, NZ), f32),
            pltpu.VMEM((2, 2, WX // 2, 8, NZ), f32),
            pltpu.VMEM((2, 2, WX // 2, 8, NZ), f32),
            pltpu.VMEM((2, 4, 8, NZ), f32),
            pltpu.VMEM((7, WIDE - 2, 24, NZ), f32),
            pltpu.VMEM(wide, f32),
            pltpu.VMEM(wide, f32),
            pltpu.VMEM(wide, f32),
            pltpu.VMEM(wide, f32),
            pltpu.VMEM((2, 8, 128), f32),
            pltpu.VMEM((NGX, 8, 128), f32),
            pltpu.VMEM((NGY, 8, 128), f32),
            dma((10,)), dma((10,)), dma((2, 8)), dma((2, 8)),
            dma((NGX,)), dma((NGX,)), dma((NGY,)), dma((NGY,)),
        ],
        compiler_params=pltpu.CompilerParams(
            collective_id=0, has_side_effects=True, vmem_limit_bytes=48 << 20
        ),
        name="coupling",
    )(counts, columns, layers, data, source)


def shards(part_column, part_layer, part_count, part_data, source):
    return run(part_count, part_column[0], part_layer[0], part_data[0], source)


def solution(mesh):
    placed = (
        P(("gx", "gy"), None, None),
        P(("gx", "gy"), None, None),
        P(("gx", "gy"), None),
        P(("gx", "gy"), None, None, None),
        P("gx", "gy", None),
    )
    return jax.shard_map(
        shards,
        mesh=mesh,
        in_specs=placed,
        out_specs=(P("gx", "gy", None), P(None, "gx", "gy", None), P("gx", "gy", None)),
        check_vma=False,
    )
```

```python
import jax
import jax.numpy as jnp
from jax import lax
from jax.experimental import pallas as pl
from jax.experimental.pallas import tpu as pltpu
from jax.sharding import PartitionSpec as P

diag_shift = 0.01
WX, WY, NZ, CAP = 16, 8, 256, 256
NGX, NGY = 8, 16
MAIN = (WX + 1) * 4 * WY
ROWS = MAIN + 80
VALUES = 9
f32, bf16 = jnp.float32, jnp.bfloat16
MESH = pl.DeviceIdType.MESH


def tables(slot, k):
    part = [slot[k, :, CAP * i : CAP * (i + 1)] for i in range(VALUES)]
    ox, oy, oz = part[:3]
    column = part[7].astype(jnp.int32)
    bx, by = column >> 3, column & 7
    xi = lax.broadcasted_iota(jnp.int32, (72, CAP), 0) >> 2
    fi = lax.broadcasted_iota(jnp.int32, (8, CAP), 0) & 3
    loads = jnp.where(fi == 0, part[3], jnp.where(fi == 1, part[4], jnp.where(fi == 2, part[5], part[6])))
    wx = jnp.where(bx == xi, 1.0 - ox, jnp.where(bx + 1 == xi, ox, 0.0))
    xf = (wx.reshape(9, 8, CAP) * loads[None]).reshape(72, CAP)
    yi = lax.broadcasted_iota(jnp.int32, (8, CAP), 0)
    wy = jnp.where(by == yi, 1.0 - oy, jnp.where(by + 1 == yi, oy, 0.0))
    over = jnp.where(by == 7, oy, 0.0)
    main = (xf[:68, None, :] * wy[None]).reshape(MAIN, CAP)
    left = jnp.concatenate([main, xf * over, jnp.zeros((8, CAP), f32)], 0)
    high = left.astype(bf16)
    low = (left - high.astype(f32)).astype(bf16)
    q = jnp.round(oz * 256.0) * (1.0 / 256.0)
    e = oz - q
    zi = lax.broadcasted_iota(jnp.int32, (NZ, CAP), 0).astype(f32).astype(bf16)
    here = zi == part[8].astype(bf16)
    above = zi == jnp.where(part[8] == NZ - 1.0, 0.0, part[8] + 1.0).astype(bf16)
    zero = jnp.zeros((), bf16)
    rest = e.astype(bf16)
    z_high = jnp.where(here, (1.0 - q).astype(bf16), jnp.where(above, q.astype(bf16), zero))
    z_low = jnp.where(here, -rest, jnp.where(above, rest, zero))
    return high, low, z_high, z_low


def dot_nt(a, b):
    return lax.dot_general(a, b, (((1,), (1,)), ((), ())), preferred_element_type=f32)


GROUP = 8
HALO = 3
WIDE = WX + 2 * HALO
AHEAD = 4
DEVICES = NGX * NGY


def kernel(
    counts, columns, layers, data, source, porosity_out, drag_out, pressure_out,
    packed, slots, total, ready, all_send, all_recv,
    over_x, over_y, over_c, next_x, diag_y, diag_x, cross_y, cross_x, tip, f_send, f_recv, y_send, y_recv, corner, face, poro, u0, u1, u2,
    red, red_x, red_y, edge_send, edge_recv, halo_send, halo_recv, rx_send, rx_recv, ry_send, ry_recv,
):
    gx, gy = lax.axis_index("gx"), lax.axis_index("gy")
    xp, xm = lax.rem(gx + 1, NGX), lax.rem(gx + NGX - 1, NGX)
    yp, ym = lax.rem(gy + 1, NGY), lax.rem(gy + NGY - 1, NGY)

    near = NGX + NGY - 1

    def peer(k):
        if isinstance(k, int) and k < near:
            step_x, step_y = (k, 0) if k < NGX else (0, k - NGX + 1)
        else:
            step_x, step_y = 1 + lax.rem(k - near, NGX - 1), 1 + lax.div(k - near, NGX - 1)
        return lax.rem(gx + step_x, NGX), lax.rem(gy + step_y, NGY)

    barrier = pltpu.get_barrier_semaphore()
    for k in range(1, near):
        pl.semaphore_signal(barrier, inc=1, device_id=peer(k), device_id_type=MESH)

    lane = lax.broadcasted_iota(jnp.int32, (1, CAP), 1)

    def pack(target, k, d):
        live = lane < counts[0, d]
        rows = data[d]
        for i in range(7):
            row = rows[i : i + 1]
            target[k, :, CAP * i : CAP * (i + 1)] = row if i < 3 else jnp.where(live, row, 0.0)
        target[k, :, CAP * 7 : CAP * 8] = columns[pl.ds(d, 1)].astype(f32)
        target[k, :, CAP * 8 :] = layers[pl.ds(d, 1)].astype(f32)

    def pack_one(k):
        px, py = peer(k)
        pack(packed, k, px * NGY + py)

    for k in range(1, near):
        pack_one(k)
    pack(slots, 0, gx * NGY + gy)

    def ship(group, g):
        k = group * GROUP + g
        pltpu.make_async_remote_copy(
            src_ref=packed.at[k],
            dst_ref=slots.at[k],
            send_sem=all_send,
            recv_sem=all_recv.at[group],
            device_id=peer(k),
            device_id_type=MESH,
        ).start()

    pl.semaphore_wait(barrier, near - 1)
    for k in range(1, NGY):
        pl.semaphore_signal(ready, inc=1, device_id=(gx, lax.rem(gy + k, NGY)), device_id_type=MESH)
    for k in range(1, near):
        ship(k // GROUP, k % GROUP)
    for k in range(near, AHEAD * GROUP):
        pack_one(k)
    pl.semaphore_wait(ready, NGY - 1)
    for k in range(near, AHEAD * GROUP):
        ship(k // GROUP, k % GROUP)

    def arrived(group, first, count):
        block = slots.at[pl.ds(first, count)]
        pltpu.make_async_copy(block, block, all_recv.at[group]).wait()

    def add_group(i):
        left, right = [], []
        for g in range(GROUP):
            high, low, z_high, z_low = tables(slots, i * GROUP + g)
            left += [high, low, high]
            right += [z_high, z_high, z_low]
        return dot_nt(jnp.concatenate(left, 1), jnp.concatenate(right, 1))

    total[...] = jnp.zeros_like(total)

    def step(i, shipping):
        @pl.when(i == 0)
        def _():
            arrived(0, 1, GROUP - 1)

        @pl.when(i > 0)
        def _():
            arrived(i, i * GROUP, GROUP)

        if shipping:
            for g in range(GROUP):
                pack_one((i + AHEAD) * GROUP + g)
                ship(i + AHEAD, g)
        total[...] += add_group(i)

    groups = DEVICES // GROUP
    lax.fori_loop(0, groups - AHEAD, lambda i, c: (step(i, True), c)[1], 0)
    lax.fori_loop(groups - AHEAD, groups, lambda i, c: (step(i, False), c)[1], 0)
    shipped = packed.at[pl.ds(1, DEVICES - 1)]
    pltpu.make_async_copy(shipped, shipped, all_send).wait()

    def send(src, dst, send_sem, recv_sem, to):
        copy = pltpu.make_async_remote_copy(
            src_ref=src, dst_ref=dst, send_sem=send_sem, recv_sem=recv_sem, device_id=to, device_id_type=MESH
        )
        copy.start()
        return copy

    top, side = 4 * WX * WY, 4 * WX
    ends = total[top:MAIN].reshape(4, 8, NZ)
    tip[...] = jnp.concatenate([ends[:, 7], ends[:, 0]], 0)
    blocks = total[:top].reshape(WX, 4, 8, NZ)
    for i, y in enumerate((7, 0)):
        f_send[i, 0] = blocks[:, 0, y]
        f_send[i, 1] = blocks[:, 2, y]
    routes = [
        (total.at[pl.ds(MAIN + side - 8, 16)], diag_y, (xp, yp)),
        (tip, diag_x, (xp, yp)),
        (total.at[pl.ds(MAIN, 8)], cross_y, (xm, yp)),
        (tip, cross_x, (xp, ym)),
        (total.at[pl.ds(MAIN, side + 8)], over_y, (gx, yp)),
        (f_send.at[0], f_recv.at[0], (gx, yp)),
        (f_send.at[1], f_recv.at[1], (gx, ym)),
        (total.at[pl.ds(top - 32, 64)], over_x, (xp, gy)),
        (total.at[pl.ds(MAIN + side, 8)], over_c, (xp, gy)),
        (total.at[pl.ds(0, 16)], next_x, (xm, gy)),
    ]
    edges = [send(src, dst, edge_send.at[i], edge_recv.at[i], to) for i, (src, dst, to) in enumerate(routes)]
    for copy in edges:
        copy.wait()

    from_y = jnp.concatenate([over_y[:8] + diag_y[8:], over_y[8:side]], 0)
    inner = total[:top].reshape(side, 8, NZ)
    inner = jnp.concatenate([inner[:4] + over_x[32:].reshape(4, 8, NZ), inner[4:]], 0)
    row = lax.broadcasted_iota(jnp.int32, (side, 8, NZ), 1)
    inner = inner + jnp.where(row == 0, from_y[:, None, :], 0.0)
    inner = inner.reshape(WX, 4, 8, NZ)
    porosity = 1.0 / (1.0 + inner[:, 0])
    drag = [inner[:, 1], inner[:, 2], inner[:, 3]]
    porosity_out[...] = porosity
    for m in range(3):
        drag_out[m] = drag[m]

    own_x, own_y = pl.ds(HALO, WX), pl.ds(8, 8)

    def send_halo(k, ref):
        pair = ref[own_x, own_y].reshape(WX // 2, 2, 8, NZ)
        even, odd = pair[:, 0], pair[:, 1]
        upper_half = lax.broadcasted_iota(jnp.int32, (WX // 2, 8, NZ), 1) >= 4
        y_send[k, 0] = jnp.where(upper_half, odd, pltpu.roll(even, 4, 1))
        y_send[k, 1] = jnp.where(upper_half, pltpu.roll(odd, 4, 1), even)
        last = WX // 2 - 1

        def put(i, src, dst, to):
            return send(src, dst, halo_send.at[k, i], halo_recv.at[k, i], to)

        return [
            put(0, y_send.at[k, 0, last], corner.at[k, 0], (xp, yp)),
            put(1, y_send.at[k, 1, last], corner.at[k, 1], (xp, ym)),
            put(2, y_send.at[k, 0, 0], corner.at[k, 2], (xm, yp)),
            put(3, y_send.at[k, 1, 0], corner.at[k, 3], (xm, ym)),
            put(4, y_send.at[k, 0], y_recv.at[k, 0], (gx, yp)),
            put(5, y_send.at[k, 1], y_recv.at[k, 1], (gx, ym)),
            put(6, ref.at[pl.ds(WX, HALO), own_y], ref.at[pl.ds(0, HALO), own_y], (xp, gy)),
            put(7, ref.at[pl.ds(HALO, HALO), own_y], ref.at[pl.ds(WX + HALO, HALO), own_y], (xm, gy)),
        ]

    def place_faces(k, ref):
        low, high = y_recv[k, 0], y_recv[k, 1]
        ref[own_x, :8] = jnp.stack([pltpu.roll(low, 4, 1), low], 1).reshape(WX, 8, NZ)
        ref[own_x, 16:] = jnp.stack([high, pltpu.roll(high, 4, 1)], 1).reshape(WX, 8, NZ)

    def place_corners(k, ref):
        for i, x in ((0, 1), (2, WX + HALO)):
            low, high = corner[k, i], corner[k, i + 1]
            ref[x, :8] = pltpu.roll(low, 4, 0)
            ref[x + 1, :8] = low
            ref[x, 16:] = high
            ref[x + 1, 16:] = pltpu.roll(high, 4, 0)

    poro[own_x, own_y] = porosity
    halo = send_halo(0, poro)

    first_y = lax.broadcasted_iota(jnp.int32, (2, 8, NZ), 1) == 0
    below_x = over_x[:16].reshape(2, 8, NZ) + jnp.where(first_y, diag_y[4:6][:, None, :], 0.0)
    above_x = next_x[...].reshape(2, 8, NZ) + total[top : top + 16].reshape(2, 8, NZ)
    above_x = above_x + jnp.where(first_y, (cross_y[:2] + over_y[side : side + 2])[:, None, :], 0.0)
    first_x = lax.broadcasted_iota(jnp.int32, (WX, NZ), 0) == 0
    mine = total[MAIN : MAIN + side].reshape(WX, 4, NZ)
    below_y, above_y = [], []
    for i, f in enumerate((0, 2)):
        below_y.append(f_recv[0, i] + jnp.where(first_x, diag_x[f : f + 1], 0.0))
        corner_sum = cross_x[4 + f : 5 + f] + over_c[f : f + 1]
        above_y.append(f_recv[1, i] + mine[:, f] + jnp.where(first_x, corner_sum, 0.0))

    yi = lax.broadcasted_iota(jnp.int32, (WX, 8, NZ), 1)

    def z_next(v):
        return pltpu.roll(v, NZ - 1, 2)

    def z_previous(v):
        return pltpu.roll(v, 1, 2)

    def step_y(v, low, high):
        return jnp.where(yi == 7, high, pltpu.roll(v, 7, 1)), jnp.where(yi == 0, low, pltpu.roll(v, 1, 1))

    def step_x(v, low, high):
        return jnp.concatenate([v[1:], high[None]], 0), jnp.concatenate([low[None], v[: WX - 1]], 0)

    after, before = step_y(drag[1], below_y[1][:, None, :], above_y[1][:, None, :])
    x_after, x_before = step_x(drag[0], below_x[1], above_x[1])
    divergence = 0.5 * (x_after - x_before)
    divergence = divergence + 0.5 * (after - before)
    divergence = divergence + 0.5 * (z_next(drag[2]) - z_previous(drag[2]))
    right_side = source[...] - divergence
    low, high = 1.0 / (1.0 + below_y[0]), 1.0 / (1.0 + above_y[0])
    after, before = step_y(porosity, low[:, None, :], high[:, None, :])
    x_after, x_before = step_x(porosity, 1.0 / (1.0 + below_x[0]), 1.0 / (1.0 + above_x[0]))

    def precondition(p, x_after, x_before, y_after, y_before):
        x_upper, x_lower = 0.5 * (p + x_after), 0.5 * (x_before + p)
        y_upper, y_lower = 0.5 * (p + y_after), 0.5 * (y_before + p)
        z_upper = 0.5 * (p + z_next(p))
        z_lower = z_previous(z_upper)
        weights = (x_upper, x_lower, y_upper, y_lower, z_upper, z_lower)
        return weights, 1.0 / (diag_shift + x_upper + x_lower + y_upper + y_lower + z_upper + z_lower)

    start = precondition(porosity, x_after, x_before, after, before)[1] * right_side
    u0[own_x, own_y] = start
    more = send_halo(1, u0)

    for copy in halo:
        copy.wait()
    place_faces(0, poro)
    place_corners(0, poro)

    def y_steps(v):
        return pltpu.roll(v, 23, 1), pltpu.roll(v, 1, 1)

    p = poro[1 : WIDE - 1]
    weights, precond = precondition(p, poro[2:], poro[: WIDE - 2], *y_steps(p))
    for i, w in enumerate(weights + (precond,)):
        face[i] = w
    for copy in more:
        copy.wait()
    place_faces(1, u0)
    place_corners(1, u0)

    def operate(ref, low):
        high = WIDE - low
        v = ref[low:high]
        w = [face[i, low - 1 : high - 1] for i in range(6)]
        y_after, y_before = y_steps(v)
        result = diag_shift * v
        result = result + w[0] * (v - ref[low + 1 : high + 1])
        result = result + w[1] * (v - ref[low - 1 : high - 1])
        result = result + w[2] * (v - y_after)
        result = result + w[3] * (v - y_before)
        result = result + w[4] * (v - z_next(v))
        return result + w[5] * (v - z_previous(v))

    def partial_sum(a, b):
        product = jnp.sum(a * b, 0)
        return jnp.sum(product[:, :128] + product[:, 128:], 0, keepdims=True)

    a0 = operate(u0, 1)
    u1[1 : WIDE - 1] = face[6] * a0
    a1 = operate(u1, 2)
    u2[2 : WIDE - 2] = face[6, 1 : WX + 3] * a1
    v2 = u2[own_x, own_y]
    w = [face[i, HALO - 1 : HALO - 1 + WX, 8:16] for i in range(6)]
    y_after, y_before = step_y(v2, u2[own_x, 7:8], u2[own_x, 16:17])
    a2 = diag_shift * v2
    a2 = a2 + w[0] * (v2 - u2[pl.ds(HALO + 1, WX), own_y])
    a2 = a2 + w[1] * (v2 - u2[pl.ds(HALO - 1, WX), own_y])
    a2 = a2 + w[2] * (v2 - y_after)
    a2 = a2 + w[3] * (v2 - y_before)
    a2 = a2 + w[4] * (v2 - z_next(v2))
    a2 = a2 + w[5] * (v2 - z_previous(v2))
    a0, a1 = a0[2 : WX + 2, 8:16], a1[1 : WX + 1, 8:16]
    v1 = u1[own_x, own_y]
    moments = [
        partial_sum(right_side, start),
        partial_sum(start, a0),
        partial_sum(v1, a0),
        partial_sum(v1, a1),
        partial_sum(v2, a1),
        partial_sum(v2, a2),
    ]

    zero = jnp.zeros((2, 128), f32)
    mine = jnp.concatenate(moments + [zero], 0)
    red[0] = mine
    red_x[gx] = mine
    copies = [
        send(red.at[0], red_x.at[gx], rx_send.at[k], rx_recv.at[k], (lax.rem(gx + k, NGX), gy)) for k in range(1, NGX)
    ]
    for copy in copies:
        copy.wait()
    mine = jnp.sum(red_x[...], 0)
    red[1] = mine
    red_y[gy] = mine
    copies = [
        send(red.at[1], red_y.at[gy], ry_send.at[k], ry_recv.at[k], (gx, lax.rem(gy + k, NGY))) for k in range(1, NGY)
    ]
    for copy in copies:
        copy.wait()
    sums = jnp.sum(jnp.sum(red_y[...], 0), 1, keepdims=True)
    m0, m1, m2, m3, m4, m5 = [sums[i : i + 1] for i in range(6)]
    l21, l31 = m2 / m1, m3 / m1
    d2 = m3 - l21 * m2
    e32 = m4 - l31 * m2
    r1 = m1 - l21 * m0
    r2 = m2 - l31 * m0
    l32 = jnp.where(d2 > 1e-8 * m3, e32 / d2, 0.0)
    d3 = (m5 - l31 * m3) - l32 * e32
    c2 = jnp.where(d3 > 1e-8 * m5, (r2 - l32 * r1) / d3, 0.0)
    c1 = jnp.where(d2 > 1e-8 * m3, r1 / d2 - l32 * c2, 0.0)
    c0 = m0 / m1 - l21 * c1 - l31 * c2
    c0, c1, c2 = [c.reshape(1, 1, 1) for c in (c0, c1, c2)]
    pressure_out[...] = c0 * u0[own_x, own_y] + c1 * u1[own_x, own_y] + c2 * u2[own_x, own_y]


def run(counts, columns, layers, data, source):
    vmem = pl.BlockSpec(memory_space=pltpu.VMEM)
    block = (WX, WY, NZ)
    wide = (WIDE, 24, NZ)
    dma = pltpu.SemaphoreType.DMA
    return pl.pallas_call(
        kernel,
        out_shape=(
            jax.ShapeDtypeStruct(block, f32),
            jax.ShapeDtypeStruct((3,) + block, f32),
            jax.ShapeDtypeStruct(block, f32),
        ),
        in_specs=[pl.BlockSpec(memory_space=pltpu.SMEM), vmem, vmem, vmem, vmem],
        out_specs=(vmem, vmem, vmem),
        scratch_shapes=[
            pltpu.VMEM((DEVICES, 1, VALUES * CAP), f32),
            pltpu.VMEM((DEVICES, 1, VALUES * CAP), f32),
            pltpu.VMEM((ROWS, NZ), f32),
            pltpu.SemaphoreType.REGULAR, dma(()), dma((DEVICES // GROUP,)),
            pltpu.VMEM((64, NZ), f32),
            pltpu.VMEM((72, NZ), f32),
            pltpu.VMEM((8, NZ), f32),
            pltpu.VMEM((16, NZ), f32),
            pltpu.VMEM((16, NZ), f32),
            pltpu.VMEM((8, NZ), f32),
            pltpu.VMEM((8, NZ), f32),
            pltpu.VMEM((8, NZ), f32),
            pltpu.VMEM((8, NZ), f32),
            pltpu.VMEM((2, 2, WX, NZ), f32),
            pltpu.VMEM((2, 2, WX, NZ), f32),
            pltpu.VMEM((2, 2, WX // 2, 8, NZ), f32),
            pltpu.VMEM((2, 2, WX // 2, 8, NZ), f32),
            pltpu.VMEM((2, 4, 8, NZ), f32),
            pltpu.VMEM((7, WIDE - 2, 24, NZ), f32),
            pltpu.VMEM(wide, f32),
            pltpu.VMEM(wide, f32),
            pltpu.VMEM(wide, f32),
            pltpu.VMEM(wide, f32),
            pltpu.VMEM((2, 8, 128), f32),
            pltpu.VMEM((NGX, 8, 128), f32),
            pltpu.VMEM((NGY, 8, 128), f32),
            dma((10,)), dma((10,)), dma((2, 8)), dma((2, 8)),
            dma((NGX,)), dma((NGX,)), dma((NGY,)), dma((NGY,)),
        ],
        compiler_params=pltpu.CompilerParams(
            collective_id=0, has_side_effects=True, vmem_limit_bytes=48 << 20
        ),
        name="coupling",
    )(counts, columns, layers, data, source)


def shards(part_column, part_layer, part_count, part_data, source):
    return run(part_count, part_column[0], part_layer[0], part_data[0], source)


def solution(mesh):
    placed = (
        P(("gx", "gy"), None, None),
        P(("gx", "gy"), None, None),
        P(("gx", "gy"), None),
        P(("gx", "gy"), None, None, None),
        P("gx", "gy", None),
    )
    return jax.shard_map(
        shards,
        mesh=mesh,
        in_specs=placed,
        out_specs=(P("gx", "gy", None), P(None, "gx", "gy", None), P("gx", "gy", None)),
        check_vma=False,
    )
```
